256 devices in a mesh: inst: 64 (over z_lo, y, x), tp: 4 (over z_hi, core).
Axes of the slice: x: 4, y: 4, z: 8 (z_hi: 2, z_lo: 4; z = z_hi * 4 + z_lo), core: 2. Of those that a mesh axis runs over, the one named last changes fastest.
Arguments:
- pool_kv: bfloat16 [3072, 2, 8, 64, 128], P('inst', None, 'tp'), may hold values from -6 to 6
- block_table: int32 [256, 24], P('inst'), may hold values from 0 to 47
- context_len: int32 [64, 4], replicated, may hold values from 1 to 1536, 3840 in all within a row
- partner: int32 [64], replicated, may hold values from 0 to 63, as said below
- mig_slot: int32 [64], replicated, may hold values from 0 to 3
- prompt_kv: bfloat16 [3072, 2, 8, 64, 128], P(('inst', 'tp')), may hold values from -6 to 6
- prompt_dest: int32 [3072, 1], replicated, may hold values from 0 to 63; in each aligned block of 48 rows (0 to 47, 48 to 95, ...) at most 2 rows name the same one
- queries: bfloat16 [320, 4, 64, 128], P('inst', None, 'tp'), may hold values from -15 to 15
- step_kv: bfloat16 [320, 4, 2, 8, 128], P('inst', None, None, 'tp'), may hold values from -6 to 6
Outputs:
- attn_out: bfloat16 [320, 4, 64, 128], P('inst', None, 'tp')
The draws below stay inside these ranges and needn't reach their ends.
Inputs may be any that keep to these rules, and one draw needn't show every extreme that they name: partner[partner[i]] = i; partner[i] differs from i in exactly one of the three lowest bits. `context_len`: each instance's 4 lengths sum to 3840. `prompt_dest`: among the 48 prompt pages held by one instance, no instance is named more than 2 times.
All inputs are finite; a program needn't handle non-finite values.
Results may differ from the reference program's by a relative error of at most 0.0066.
Values may be sent and summed in bfloat16 or wider, within the bound.
A program may use at most 128 MiB of HBM per device.

```python
import math
import jax
import jax.numpy as jnp
import numpy as np
from jax import lax

HEADS = 64
KVH = 8
HD = 128
GROUP = 8
BLK = 64
STEPS = 4
CAP = 2
REQ_DEV = 4
MAXBLK = 24
POOL = 48
MAXLEN = 1536
TOTAL_LEN = 3840
PR_DEV = 12
PROMPTS = 3072
REQS = 320
N_INST = 64
N_TP = 4


def cube_matchings():
    collected = []

    def extend(assigned):
        unmatched = [vertex for vertex in range(8) if assigned[vertex] < 0]
        if len(unmatched) == 0:
            collected.append(list(assigned))
            return
        vertex = unmatched[0]
        for which_bit in range(3):
            other = vertex ^ 1 << which_bit
            if assigned[other] < 0:
                following = list(assigned)
                following[vertex] = which_bit
                following[other] = which_bit
                extend(following)
    extend([-1] * 8)
    return np.array(collected, dtype=np.int32)


def draw_partner(key, part):
    key = jax.random.fold_in(key, 11)
    table = jnp.asarray(cube_matchings())
    groups = N_INST // 8
    picked = jax.random.randint(key, (groups,), 0, table.shape[0])
    spread = table[picked].reshape(-1)
    index = jnp.arange(N_INST, dtype=jnp.int32)
    return jnp.bitwise_xor(index, jnp.left_shift(1, spread)).astype(jnp.int32)


def draw_pool_kv(key, part):
    own = jax.random.fold_in(key, 21)
    shape = (N_INST * POOL, 2, KVH, BLK, HD)
    base = jnp.clip(jax.random.normal(own, shape, jnp.float32), -6.0, 6.0)
    return base.astype(jnp.bfloat16)


def draw_prompt_kv(key, part):
    own = jax.random.fold_in(key, 31)
    shape = (PROMPTS, 2, KVH, BLK, HD)
    base = jnp.clip(jax.random.normal(own, shape, jnp.float32), -6.0, 6.0)
    return base.astype(jnp.bfloat16)


def draw_queries(key, part):
    own = jax.random.fold_in(key, 41)
    shape = (REQS, STEPS, HEADS, HD)
    base = jnp.clip(2.5 * jax.random.normal(own, shape, jnp.float32), -15.0, 15.0)
    return base.astype(jnp.bfloat16)


def draw_step_kv(key, part):
    own = jax.random.fold_in(key, 51)
    shape = (REQS, STEPS, 2, KVH, HD)
    base = jnp.clip(jax.random.normal(own, shape, jnp.float32), -6.0, 6.0)
    return base.astype(jnp.bfloat16)


def with_ends(values, own_key, smallest, largest):
    place = [jax.random.randint(jax.random.fold_in(own_key, axis), (), 0, length) for axis, length in enumerate(values.shape)]
    longest = values.shape.index(max(values.shape))
    neighbour = place[:longest] + [(place[longest] + 1) % values.shape[longest]] + place[longest + 1:]
    return values.at[tuple(place)].set(smallest).at[tuple(neighbour)].set(largest)


def length_profile(number_of, total, bound, lean):
    loads = [(1 << 20) // math.isqrt(grade ** lean) + 1 for grade in range(2, number_of + 1)]
    spare, given = total - bound - (number_of - 1), [1] * (number_of - 1)
    while spare > 0:
        candidates = [i for i in range(number_of - 1) if given[i] < bound]
        mass, left = sum([loads[i] for i in candidates]), spare
        for i in candidates:
            addition = min(bound - given[i], max(1, left * loads[i] // mass), spare)
            given[i] = given[i] + addition
            spare = spare - addition
    return np.array([bound] + given)


def ragged(rng, number_of, total, most, skew):
    if number_of == 2:
        one = jax.random.randint(rng, (), max(1, total - most), min(most, total - 1) + 1)
        return jnp.stack([one, total - one])
    sizes = jnp.asarray(length_profile(number_of, total, most, skew), jnp.int32)
    pairs = (number_of - 1) // 2
    donor, sink = sizes[1:1 + 2 * pairs:2], sizes[2:2 + 2 * pairs:2]
    margin = jnp.minimum(donor - 1, most - sink)
    moved = jax.random.randint(jax.random.fold_in(rng, 1), (pairs,), 0, 1 << 20) % (margin + 1)
    sizes = sizes.at[1:1 + 2 * pairs:2].set(donor - moved).at[2:2 + 2 * pairs:2].set(sink + moved)
    return sizes[jax.random.permutation(jax.random.fold_in(rng, 2), number_of)]


def shared_out(rng, own, number, rows, number_of, top, limit, lean):
    ranking = jax.random.permutation(rng, number_of)
    crowded, usual = load_shares(number_of, rows * top, limit, lean, True), load_shares(number_of, rows * top, limit, lean, False)
    places = jnp.arange(number_of)

    def named(sizes, rotation):
        used = int((sizes > 0).sum())
        fixed = max(1, used // 4)
        shifted = fixed + (places - fixed + rotation * (used - fixed)) % max(1, number_of - fixed)
        return jnp.zeros((number_of,), jnp.int32).at[ranking[jnp.where(places < fixed, places, shifted)]].set(jnp.asarray(sizes, jnp.int32))

    sizes = jnp.where(number % 4 == 0, named(crowded, number // 4), named(usual, number - number // 4 - 1))
    mixed = jax.random.permutation(jax.random.fold_in(own, 3), number_of)
    donor, receiver = mixed[0:number_of // 2 * 2:2], mixed[1:number_of // 2 * 2:2]
    margin = jnp.minimum(sizes[donor] - 1, limit - sizes[receiver]) // 2
    margin = jnp.where((donor == ranking[0]) | (receiver == ranking[0]) | (sizes[receiver] == 0), 0, jnp.maximum(margin, 0))
    shifted = jax.random.randint(jax.random.fold_in(own, 4), (number_of // 2,), 0, 1 << 20) % (margin + 1)
    sizes = sizes.at[donor].add(-shifted).at[receiver].add(shifted)
    labels = jnp.searchsorted(jnp.cumsum(sizes), jnp.arange(rows * top), side="right").astype(jnp.int32)
    grid = labels.reshape(top, rows).T
    grid = grid[jax.random.permutation(jax.random.fold_in(own, 1), rows)]
    rotation = jax.random.randint(jax.random.fold_in(own, 2), (rows, 1), 0, top)
    return jnp.take_along_axis(grid, (jnp.arange(top)[None, :] + rotation) % top, axis=1)


def load_shares(number_of, total, limit, skew, full):
    portions = [(1 << 20) // math.isqrt(standing ** skew) + 1 for standing in range(1, number_of + 1)]
    largest = limit if full else min(limit, max(-(-total // number_of), total * portions[0] // sum(portions)))
    least = 1 if total - largest >= number_of - 1 else 0
    holding, rest = [largest] + [least] * (number_of - 1), total - largest - least * (number_of - 1)
    while rest > 0:
        free = [i for i in range(1, number_of) if holding[i] < largest] or [i for i in range(1, number_of) if holding[i] < limit]
        mass, remaining = sum([portions[i] for i in free]), rest
        for i in free:
            extra = min(limit - holding[i], max(1, remaining * portions[i] // mass), rest)
            holding[i] = holding[i] + extra
            rest = rest - extra
    return np.array(holding)


def setup_inputs(seed: int = 0) -> dict:
    seeds = jax.random.split(jax.random.key(seed), 10)
    pool_kv = draw_pool_kv(jax.random.fold_in(seeds[9], 71), 0)
    block_table = with_ends(jax.random.randint(seeds[1], (N_INST * REQ_DEV, MAXBLK), 0, POOL), jax.random.fold_in(seeds[1], 1), 0, POOL - 1).astype(jnp.int32)
    context_len = jax.vmap(lambda own: ragged(own, REQ_DEV, TOTAL_LEN, MAXLEN, 2))(jax.random.split(seeds[2], N_INST)).reshape((N_INST, REQ_DEV)).astype(jnp.int32)
    partner = draw_partner(jax.random.fold_in(seeds[9], 71), 0)
    mig_slot = with_ends(jax.random.randint(seeds[4], (N_INST,), 0, REQ_DEV), jax.random.fold_in(seeds[4], 1), 0, REQ_DEV - 1).astype(jnp.int32)
    prompt_kv = draw_prompt_kv(jax.random.fold_in(seeds[9], 71), 0)
    prompt_dest_keys = jax.random.split(jax.random.fold_in(seeds[6], 1), PROMPTS // (N_TP * PR_DEV))
    prompt_dest_turns = jax.random.permutation(jax.random.fold_in(seeds[6], 3), PROMPTS // (N_TP * PR_DEV))
    prompt_dest = jax.vmap(lambda own, number: shared_out(jax.random.fold_in(seeds[6], 2), own, number, N_TP * PR_DEV, N_INST, 1, CAP, 2))(prompt_dest_keys, prompt_dest_turns).reshape((PROMPTS, 1))
    queries = draw_queries(jax.random.fold_in(seeds[9], 71), 0)
    step_kv = draw_step_kv(jax.random.fold_in(seeds[9], 71), 0)
    return {"pool_kv": pool_kv, "block_table": block_table, "context_len": context_len, "partner": partner, "mig_slot": mig_slot, "prompt_kv": prompt_kv, "prompt_dest": prompt_dest, "queries": queries, "step_kv": step_kv}


def rope_freqs(size):
    half = size // 2
    ratio = jnp.arange(half, dtype=jnp.float32) * (2.0 / size)
    base = jnp.exp(-ratio * math.log(500000.0))
    wavelength = 2.0 * math.pi / base
    smooth = (8192.0 / wavelength - 1.0) / 3.0
    blended = (1.0 - smooth) * base / 8.0 + smooth * base
    return jnp.where(wavelength < 2048.0, base, jnp.where(wavelength > 8192.0, base / 8.0, blended))

def rotate(vector, position):
    half = vector.shape[-1] // 2
    angles = position.astype(jnp.float32)[..., None] * rope_freqs(vector.shape[-1])
    cosine = jnp.cos(angles)
    sine = jnp.sin(angles)
    first = vector[..., :half]
    second = vector[..., half:]
    return jnp.concatenate([first * cosine - second * sine, second * cosine + first * sine], axis=-1)

def query_groups(query, length):
    positions = length + jnp.arange(STEPS, dtype=jnp.int32)
    turned = rotate(query.astype(jnp.float32), positions[:, None]).astype(jnp.bfloat16)
    return turned.reshape(STEPS, KVH, GROUP, HD).transpose(1, 0, 2, 3).reshape(KVH, STEPS * GROUP, HD)

def ungroup(result):
    return result.reshape(KVH, STEPS, GROUP, HD).transpose(1, 0, 2, 3).reshape(STEPS, HEADS, HD).astype(jnp.bfloat16)

def page_stats(qrot, keys, values, valid):
    scores = jnp.einsum('hrd,phtd->hrpt', qrot.astype(jnp.float32), keys.astype(jnp.float32)) / math.sqrt(HD)
    masked = jnp.where(valid, scores, -1e+30)
    top = lax.optimization_barrier(jnp.max(masked, axis=3))
    weights = jnp.where(valid, jnp.exp(masked - top[..., None]), 0.0).astype(jnp.bfloat16)
    total = lax.optimization_barrier(jnp.sum(weights.astype(jnp.float32), axis=3))
    acc = jnp.einsum('hrpt,phtd->hrpd', weights.astype(jnp.float32), values.astype(jnp.float32))
    return (top, total, acc)

def new_page(qrot, kv_steps, length):
    positions = length + jnp.arange(STEPS, dtype=jnp.int32)
    keys = rotate(kv_steps[:, 0].astype(jnp.float32), positions[:, None]).astype(jnp.bfloat16)
    keys = keys.transpose(1, 0, 2)[None]
    values = kv_steps[:, 1].transpose(1, 0, 2)[None]
    row_step = jnp.arange(STEPS * GROUP, dtype=jnp.int32) // GROUP
    valid = jnp.arange(STEPS, dtype=jnp.int32)[None, None, :] <= row_step[:, None, None]
    return page_stats(qrot, keys, values, valid)

def finish(parts):
    top = jnp.concatenate([part[0] for part in parts], axis=2)
    total = jnp.concatenate([part[1] for part in parts], axis=2)
    acc = jnp.concatenate([part[2] for part in parts], axis=2)
    best = lax.optimization_barrier(jnp.max(top, axis=2))
    scale = jnp.exp(top - best[..., None])
    numer = lax.optimization_barrier(jnp.sum(scale[..., None] * acc, axis=2))
    denom = lax.optimization_barrier(jnp.sum(scale * total, axis=2))
    return numer / denom[..., None]

def reference(pool_kv, block_table, context_len, partner, mig_slot, prompt_kv, prompt_dest, queries, step_kv):
    inst_ids = jnp.arange(N_INST, dtype=jnp.int32)
    slot_ids = jnp.arange(REQ_DEV, dtype=jnp.int32)
    moving = slot_ids[None, :] == mig_slot[:, None]
    source_inst = jnp.where(moving, partner[:, None], inst_ids[:, None]).astype(jnp.int32)
    source_slot = jnp.where(moving, mig_slot[partner][:, None], slot_ids[None, :]).astype(jnp.int32)
    lengths = context_len[source_inst, source_slot].reshape(-1)
    tables = block_table[(source_inst * REQ_DEV + source_slot).reshape(-1)] + (source_inst.reshape(-1) * POOL)[:, None]
    request_rows = (inst_ids[:, None] * (REQ_DEV + 1) + slot_ids[None, :]).reshape(-1)
    positions = jnp.arange(MAXBLK, dtype=jnp.int32)[:, None] * BLK + jnp.arange(BLK, dtype=jnp.int32)[None, :]

    def resident(index):
        length = lengths[index]
        row = request_rows[index]
        pages = pool_kv[tables[index]]
        qrot = query_groups(queries[row], length)
        cache = page_stats(qrot, pages[:, 0], pages[:, 1], positions < length)
        fresh = new_page(qrot, step_kv[row], length)
        return ungroup(finish([cache, fresh]))
    res_out = lax.map(resident, jnp.arange(N_INST * REQ_DEV, dtype=jnp.int32))
    dests = prompt_dest[:, 0]
    counts = lax.optimization_barrier(jnp.sum((dests[None, :] == inst_ids[:, None]).astype(jnp.int32), axis=1))
    new_len = counts * BLK
    new_rows = inst_ids * (REQ_DEV + 1) + REQ_DEV
    new_q = jax.vmap(query_groups)(queries[new_rows], new_len)

    def prompt_block(index):
        block = lax.dynamic_slice_in_dim(prompt_kv, index * PR_DEV, PR_DEV, 0)
        where_to = lax.dynamic_slice_in_dim(dests, index * PR_DEV, PR_DEV, 0)
        asked = new_q[where_to]

        def single(qrot, page):
            return page_stats(qrot, page[0][None], page[1][None], jnp.ones((1, BLK), dtype=bool))
        return jax.vmap(single)(asked, block)
    tops, totals, accs = lax.map(prompt_block, jnp.arange(N_INST * N_TP, dtype=jnp.int32))
    tops = tops.reshape(PROMPTS, KVH, STEPS * GROUP)
    totals = totals.reshape(PROMPTS, KVH, STEPS * GROUP)
    accs = accs.reshape(PROMPTS, KVH, STEPS * GROUP, HD)

    def dest_max(dest):
        return lax.optimization_barrier(jnp.max(jnp.where((dests == dest)[:, None, None], tops, -1e+30), axis=0))
    best = lax.map(dest_max, inst_ids)
    scale = jnp.exp(tops - best[dests])
    sums = jax.ops.segment_sum(scale * totals, dests, num_segments=N_INST)
    accsum = jax.ops.segment_sum(scale[..., None] * accs, dests, num_segments=N_INST)

    def new_request(dest):
        part = (best[dest][..., None], sums[dest][..., None], accsum[dest][:, :, None, :])
        fresh = new_page(new_q[dest], step_kv[new_rows[dest]], new_len[dest])
        return ungroup(finish([part, fresh]))
    new_out = lax.map(new_request, inst_ids)
    joined = jnp.concatenate([res_out.reshape(N_INST, REQ_DEV, STEPS, HEADS, HD), new_out[:, None]], axis=1)
    return joined.reshape(REQS, STEPS, HEADS, HD)
```

```python
import math

import jax
import jax.numpy as jnp
from jax import lax
from jax.experimental import pallas as pl
from jax.experimental.pallas import tpu as pltpu
from jax.sharding import PartitionSpec as P

MESH = pl.DeviceIdType.MESH
NEG = -1e30
F32 = jnp.float32
BF16 = jnp.bfloat16
HD = 128
SCALE = 1.0 / math.sqrt(HD)


def rope_freqs(size):
    half = size // 2
    ratio = jnp.arange(half, dtype=jnp.float32) * (2.0 / size)
    base = jnp.exp(-ratio * math.log(500000.0))
    wavelength = 2.0 * math.pi / base
    smooth = (8192.0 / wavelength - 1.0) / 3.0
    blended = (1.0 - smooth) * base / 8.0 + smooth * base
    return jnp.where(wavelength < 2048.0, base, jnp.where(wavelength > 8192.0, base / 8.0, blended))


def rotate(vector, cosine, sine):
    half = vector.shape[-1] // 2
    first = vector[..., :half]
    second = vector[..., half:]
    return jnp.concatenate(
        [first * cosine - second * sine, second * cosine + first * sine], axis=-1
    )


def dot_nt(a, b):
    return lax.dot_general(a, b, (((1,), (1,)), ((), ())), preferred_element_type=F32)


def dot_tn(a, b):
    return lax.dot_general(a, b, (((0,), (0,)), ((), ())), preferred_element_type=F32)


def body(
    scal, pdest, index, tab, meta, pack, pool_hbm, prompt_hbm, out,
    pool, pages, ab, mig_send, mig_rcv, ret_loc, ret_send, ret_rcv,
    qa, qb, acc, lse,
    sa, sb, la, lb, ra, rb, rla, rlb,
    sa2, sb2, la2, lb2, ra2, rb2, rla2, rlb2,
    s3, l3, r3, rl3, wgt, fin,
    local_sem, core_ssem, core_rsem, mig_ssem, mig_rsem, ret_ssem, ret_rsem,
    gz_ssem, gz_rsem, g2_ssem, g2_rsem, g3_ssem, g3_rsem,
    r1_ssem, r1_rsem, r2_ssem, r2_rsem, rz_ssem, rz_rsem,
):
    inst = lax.axis_index("inst")
    tp = lax.axis_index("tp")
    z_lo, y, x = inst // 16, (inst // 4) % 4, inst % 4
    z_hi, core = tp // 2, tp % 2
    z = z_hi * 4 + z_lo

    def device(zz, yy, xx, cc):
        return ((zz % 4) * 16 + yy * 4 + xx, (zz // 4) * 2 + cc)

    x_peers = [device(z, y, (x + k) % 4, core) for k in (1, 2, 3)]
    y_peers = [device(z, (y + k) % 4, x, core) for k in (1, 2, 3)]
    z_peers = [device((z + k) % 8, y, x, core) for k in range(1, 8)]
    core_peer = device(z, y, x, 1 - core)
    mig_peers = [
        device(z, y, x + 1 - 2 * (x % 2), core),
        device(z, y, (x + 2) % 4, core),
        device(z, y + 1 - 2 * (y % 2), x, core),
    ]

    barrier = pltpu.get_barrier_semaphore()
    everyone = [core_peer] + x_peers + y_peers + z_peers
    for peer in everyone:
        pl.semaphore_signal(barrier, inc=1, device_id=peer, device_id_type=MESH)

    def remote(src, dst, ssem, rsem, peer):
        return pltpu.make_async_remote_copy(
            src_ref=src, dst_ref=dst, send_sem=ssem, recv_sem=rsem,
            device_id=peer, device_id_type=MESH,
        )

    pool_copy = pltpu.make_async_copy(pool_hbm, pool, local_sem.at[0])
    pool_copy.start()
    own_copies = [
        pltpu.make_async_copy(
            prompt_hbm.at[:, :, pl.ds(hi * 4 + core * 2, 2)], pages.at[core, hi], local_sem.at[1 + hi]
        )
        for hi in range(2)
    ]
    for copy in own_copies:
        copy.start()

    my_slot = scal[0]
    bit = scal[1]
    mine = pack[4, pl.ds(0, 64)]
    qa[x, y, z] = mine[:32]
    qb[y, x, z] = mine[32:]
    mig_send[...] = pack[my_slot]

    pl.semaphore_wait(barrier, len(everyone))

    gz = []
    for k in range(7):
        gz.append(remote(qa.at[x, y, z], qa.at[x, y, z], gz_ssem.at[0, k], gz_rsem.at[0, k], z_peers[k]))
        gz.append(remote(qb.at[y, x, z], qb.at[y, x, z], gz_ssem.at[1, k], gz_rsem.at[1, k], z_peers[k]))
    for copy in gz:
        copy.start()
    mig = [remote(mig_send, mig_rcv.at[k], mig_ssem.at[k], mig_rsem.at[k], mig_peers[k]) for k in range(3)]
    for copy in mig:
        copy.start()
    core_copies = [
        remote(
            prompt_hbm.at[:, :, pl.ds(hi * 4 + (1 - core) * 2, 2)],
            pages.at[core, hi], core_ssem.at[hi], core_rsem.at[hi], core_peer,
        )
        for hi in range(2)
    ]
    for copy in core_copies:
        copy.start()

    shape = (12, 8, HD)
    row = lax.broadcasted_iota(jnp.int32, shape, 1)
    page_id = lax.broadcasted_iota(jnp.int32, shape, 0) * 4 + row % 4
    is_last = (row // 4).astype(jnp.int32)
    full = meta[pl.ds(0, 1), :]
    ab[...] = jnp.zeros(shape, F32)

    def count_step(k, carry):
        named = tab[pl.ds(k, 1), :][None]
        kind = jnp.where(k < full, 0, jnp.where(k == full, 1, 2))[None]
        hit = (page_id == named) & (is_last == kind)
        ab[...] += jnp.where(hit, 1.0, 0.0)
        return carry

    lax.fori_loop(0, 24, count_step, 0)

    for copy in gz:
        copy.wait()
    g2 = []
    for k in range(3):
        g2.append(remote(qa.at[x, y], qa.at[x, y], g2_ssem.at[0, k], g2_rsem.at[0, k], y_peers[k]))
        g2.append(remote(qb.at[y, x], qb.at[y, x], g2_ssem.at[1, k], g2_rsem.at[1, k], x_peers[k]))
    for copy in g2:
        copy.start()
    for copy in mig:
        copy.wait()
    for copy in g2:
        copy.wait()
    g3 = []
    for k in range(3):
        g3.append(remote(qa.at[x], qa.at[x], g3_ssem.at[0, k], g3_rsem.at[0, k], x_peers[k]))
        g3.append(remote(qb.at[y], qb.at[y], g3_ssem.at[1, k], g3_rsem.at[1, k], y_peers[k]))
    for copy in g3:
        copy.start()

    came = mig_rcv[bit].astype(F32)
    blocks = [jnp.where(my_slot == j, came, pack[j].astype(F32)).astype(BF16) for j in range(4)]
    fresh_kv = jnp.concatenate([block[64:80] for block in blocks], axis=0)
    q_res = [jnp.concatenate([block[h * 32 : h * 32 + 32] for block in blocks], axis=0) for h in range(2)]
    pool_copy.wait()
    rem = meta[pl.ds(1, 1), :]
    below = (lax.broadcasted_iota(jnp.int32, (64, HD), 0) < rem).astype(F32)

    def res_step(i, carry):
        named = ab[i]
        count = (named[0:4][:, None, :] + named[4:8][:, None, :] * below[None]).reshape(256, HD)
        real = count > 0.0
        after = []
        for h in range(2):
            best, total, summed = carry[3 * h : 3 * h + 3]
            keys = pool[pl.ds(i * 4, 4), 0, h].reshape(256, HD)
            values = pool[pl.ds(i * 4, 4), 1, h].reshape(256, HD)
            score = jnp.where(real, dot_nt(keys, q_res[h]) * SCALE, NEG)
            top = jnp.maximum(best, jnp.max(score, axis=0, keepdims=True))
            weight = (count * jnp.exp(score - top)).astype(BF16)
            shrink = jnp.exp(best - top)
            total = total * shrink + jnp.sum(weight.astype(F32), axis=0, keepdims=True)
            summed = summed * shrink + dot_tn(values, weight)
            after += [top, total, summed]
        return tuple(after)

    start = (jnp.full((1, HD), NEG, F32), jnp.zeros((1, HD), F32), jnp.zeros((HD, HD), F32)) * 2
    state = lax.fori_loop(0, 12, res_step, start)
    lane = lax.broadcasted_iota(jnp.int32, (64, HD), 1)
    line = lax.broadcasted_iota(jnp.int32, (64, HD), 0)
    ok_slot = (line // 16 == lane // 32) & (line % 16 < 8) & (line % 4 <= (lane % 32) // 8)
    rows = []
    for h in range(2):
        best, total, summed = state[3 * h : 3 * h + 3]
        ok = ok_slot & ((line % 8) // 4 == h)
        score = jnp.where(ok, dot_nt(fresh_kv, q_res[h]) * SCALE, NEG)
        top = jnp.maximum(best, jnp.max(score, axis=0, keepdims=True))
        weight = jnp.where(ok, jnp.exp(score - top), 0.0).astype(BF16).astype(F32)
        moved = jnp.concatenate([jnp.zeros((8, HD), F32), weight[:-8]], axis=0).astype(BF16)
        shrink = jnp.exp(best - top)
        total = total * shrink + jnp.sum(weight, axis=0, keepdims=True)
        summed = summed * shrink + dot_tn(fresh_kv, moved)
        rows.append((summed / total).T)
    for j in range(4):
        for s in range(4):
            at = j * 32 + s * 8
            ret_loc[j, s] = jnp.concatenate([rows[0][at : at + 8], rows[1][at : at + 8]], axis=0).astype(BF16)
    ret_send[...] = ret_loc[my_slot]
    ret = [remote(ret_send, ret_rcv.at[k], ret_ssem.at[k], ret_rsem.at[k], mig_peers[k]) for k in range(3)]
    for copy in ret:
        copy.start()

    for copy in own_copies + core_copies:
        copy.wait()
    for copy in g3:
        copy.wait()
    acc[24] = jnp.zeros((HD, HD), F32)
    lse[24] = jnp.full((1, HD), NEG, F32)
    key_head = lax.broadcasted_iota(jnp.int32, (256, HD), 0) // 64
    row_head = lax.broadcasted_iota(jnp.int32, (256, HD), 1) // 32
    same_head = key_head == row_head

    def query_of(d):
        zl, dy, dx = d // 16, (d // 4) % 4, d % 4
        return jnp.concatenate(
            [qa[dx, dy, zl], qb[dy, dx, zl], qa[dx, dy, zl + 4], qb[dy, dx, zl + 4]], axis=0
        )

    def page_step(i, carry):
        for src in range(2):
            n = src * 12 + i
            asked = query_of(pdest[n])
            keys = jnp.concatenate([pages[src, hi, i, 0].reshape(HD, HD) for hi in range(2)], axis=0)
            values = jnp.concatenate([pages[src, hi, i, 1].reshape(HD, HD) for hi in range(2)], axis=0)
            score = jnp.where(same_head, dot_nt(keys, asked) * SCALE, NEG)
            top = jnp.max(score, axis=0, keepdims=True)
            weight = jnp.exp(score - top).astype(BF16)
            total = jnp.sum(weight.astype(F32), axis=0, keepdims=True)
            acc[n] = dot_tn(values, weight) / total
            lse[n] = top + jnp.log(total)
        return carry

    lax.fori_loop(0, 12, page_step, 0)

    for dx in range(4):
        def place_step(t, carry, dx=dx):
            dy, zl = t // 4, t % 4
            d = zl * 16 + dy * 4 + dx
            first, second = index[0, d], index[1, d]
            lse0, lse1 = lse[first], lse[second]
            top = jnp.maximum(lse0, lse1)
            w0, w1 = jnp.exp(lse0 - top), jnp.exp(lse1 - top)
            total = w0 + w1
            both = top + jnp.log(total)
            block = acc[first] * (w0 / total) + acc[second] * (w1 / total)
            sa[dx, t] = block[:64].astype(BF16)
            sb[dy, dx * 4 + zl] = block[64:].astype(BF16)
            la[dx, pl.ds(t, 1), :] = both
            lb[dy, pl.ds(dx * 4 + zl, 1), :] = both
            return carry

        lax.fori_loop(0, 16, place_step, 0)

    r1 = []
    for k in range(3):
        to_x, to_y = (x + k + 1) % 4, (y + k + 1) % 4
        r1.append(remote(sa.at[to_x], ra.at[k], r1_ssem.at[0, k], r1_rsem.at[0, k], x_peers[k]))
        r1.append(remote(la.at[to_x], rla.at[k], r1_ssem.at[1, k], r1_rsem.at[1, k], x_peers[k]))
        r1.append(remote(sb.at[to_y], rb.at[k], r1_ssem.at[2, k], r1_rsem.at[2, k], y_peers[k]))
        r1.append(remote(lb.at[to_y], rlb.at[k], r1_ssem.at[3, k], r1_rsem.at[3, k], y_peers[k]))
    for copy in r1:
        copy.start()

    asked = query_of(inst)
    own_kv = pack[4, pl.ds(64, 16)]
    lane16 = lax.broadcasted_iota(jnp.int32, (16, HD), 1)
    line16 = lax.broadcasted_iota(jnp.int32, (16, HD), 0)
    ok = (line16 < 8) & (line16 // 4 == (lane16 % 64) // 32) & (line16 % 4 <= (lane16 % 32) // 8)
    score = jnp.where(ok, dot_nt(own_kv, asked) * SCALE, NEG)
    top = jnp.max(score, axis=0, keepdims=True)
    weight = jnp.where(ok, jnp.exp(score - top), 0.0).astype(BF16).astype(F32)
    moved = jnp.concatenate([jnp.zeros((8, HD), F32), weight[:-8]], axis=0).astype(BF16)
    total = jnp.sum(weight, axis=0, keepdims=True)
    new_acc = dot_tn(own_kv, moved) / total
    new_lse = top + jnp.log(total)

    def shares(parts):
        top = parts[0]
        for part in parts[1:]:
            top = jnp.maximum(top, part)
        weights = [jnp.exp(part - top) for part in parts]
        total = weights[0]
        for part in weights[1:]:
            total = total + part
        return [part / total for part in weights], top + jnp.log(total)

    for copy in r1:
        copy.wait()
    for side, (mine_s, mine_l, got_s, got_l, where, next_s, next_l) in enumerate((
        (sa, la, ra, rla, x, sa2, la2), (sb, lb, rb, rlb, y, sb2, lb2)
    )):
        weights, joined = shares([mine_l[where]] + [got_l[k] for k in range(3)])
        for k in range(4):
            wgt[k] = weights[k]
        for group in range(4):
            next_l[group] = jnp.concatenate([joined[group * 4 : group * 4 + 4], jnp.zeros((4, HD), F32)], axis=0)

        def merge_step(t, carry):
            block = mine_s[where, t].astype(F32) * wgt[0, pl.ds(t, 1), :]
            for k in range(3):
                block = block + got_s[k, t].astype(F32) * wgt[k + 1, pl.ds(t, 1), :]
            next_s[t // 4, t % 4] = block.astype(BF16)
            return carry

        lax.fori_loop(0, 16, merge_step, 0)

    r2 = []
    for k in range(3):
        to_x, to_y = (x + k + 1) % 4, (y + k + 1) % 4
        r2.append(remote(sa2.at[to_y], ra2.at[k], r2_ssem.at[0, k], r2_rsem.at[0, k], y_peers[k]))
        r2.append(remote(la2.at[to_y], rla2.at[k], r2_ssem.at[1, k], r2_rsem.at[1, k], y_peers[k]))
        r2.append(remote(sb2.at[to_x], rb2.at[k], r2_ssem.at[2, k], r2_rsem.at[2, k], x_peers[k]))
        r2.append(remote(lb2.at[to_x], rlb2.at[k], r2_ssem.at[3, k], r2_rsem.at[3, k], x_peers[k]))
    for copy in r2:
        copy.start()
    for copy in ret:
        copy.wait()
    back = [ret_rcv[bit, s].astype(F32) for s in range(4)]
    for j in range(4):
        for s in range(4):
            out[j, s] = jnp.where(my_slot == j, back[s], ret_loc[j, s].astype(F32)).astype(BF16)
    for copy in r2:
        copy.wait()
    joins = []
    for side, (mine_s, mine_l, got_s, got_l, where) in enumerate((
        (sa2, la2, ra2, rla2, y), (sb2, lb2, rb2, rlb2, x)
    )):
        weights, joined = shares([mine_l[where]] + [got_l[k] for k in range(3)])
        joins.append(joined)
        for zl in range(4):
            block = mine_s[where, zl].astype(F32) * weights[0][zl : zl + 1]
            for k in range(3):
                block = block + got_s[k, zl].astype(F32) * weights[k + 1][zl : zl + 1]
            s3[zl, pl.ds(side * 64, 64)] = block.astype(BF16)
    for zl in range(4):
        l3[zl] = jnp.concatenate(
            [joins[0][zl : zl + 1], joins[1][zl : zl + 1], jnp.zeros((6, HD), F32)], axis=0
        )
    rz = []
    for k in range(7):
        to = (z + k + 1) % 4
        rz.append(remote(s3.at[to], r3.at[k], rz_ssem.at[0, k], rz_rsem.at[0, k], z_peers[k]))
        rz.append(remote(l3.at[to], rl3.at[k], rz_ssem.at[1, k], rz_rsem.at[1, k], z_peers[k]))
    for copy in rz:
        copy.start()
    for copy in rz:
        copy.wait()
    new_rows = jnp.concatenate([new_lse] * 8, axis=0)
    weights, _ = shares([new_rows, l3[z_lo]] + [rl3[k] for k in range(7)])
    halves = []
    for side in range(2):
        at = pl.ds(side * 64, 64)
        block = new_acc[side * 64 : side * 64 + 64] * weights[0][side : side + 1]
        block = block + s3[z_lo, at].astype(F32) * weights[1][side : side + 1]
        for k in range(7):
            block = block + r3[k, at].astype(F32) * weights[k + 2][side : side + 1]
        halves.append(block)
    fin[...] = jnp.concatenate(halves, axis=0).T
    here = fin[pl.ds(z_hi * 64, 64), :]
    for s in range(4):
        out[4, s] = jnp.concatenate([here[s * 8 : s * 8 + 8], here[32 + s * 8 : 40 + s * 8]], axis=0).astype(BF16)


def per_device(
    pool_kv, block_table, context_len, partner, mig_slot, prompt_kv, prompt_dest, queries, step_kv
):
    inst = lax.axis_index("inst")
    tp = lax.axis_index("tp")
    my_slot = mig_slot[inst]
    mate = partner[inst]
    mate_len = context_len[mate, mig_slot[mate]]
    own_len = context_len[inst]
    post_len = jnp.where(jnp.arange(4, dtype=jnp.int32) == my_slot, mate_len, own_len)
    dests = prompt_dest[:, 0]
    new_len = jnp.sum((dests == inst).astype(jnp.int32)) * 64
    lens = jnp.concatenate([post_len, new_len[None]])
    positions = lens[:, None] + jnp.arange(4, dtype=jnp.int32)
    angles = positions.astype(F32)[..., None] * rope_freqs(HD)
    cosine, sine = jnp.cos(angles)[:, :, None], jnp.sin(angles)[:, :, None]
    qrot = rotate(queries.astype(F32), cosine, sine).astype(BF16)
    qrot = qrot.reshape(5, 4, 2, 8, HD).transpose(0, 2, 1, 3, 4).reshape(5, 64, HD)
    knew = rotate(step_kv[:, :, 0].astype(F32), cosine, sine).astype(BF16)
    knew = knew.transpose(0, 2, 1, 3).reshape(5, 8, HD)
    vnew = step_kv[:, :, 1].transpose(0, 2, 1, 3).reshape(5, 8, HD)
    pack = jnp.concatenate([qrot, knew, vnew], axis=1)

    gap = jnp.bitwise_xor(inst, mate)
    bit = jnp.where(gap == 1, 0, jnp.where(gap == 2, 1, 2))
    scal = jnp.stack([my_slot, bit]).astype(jnp.int32)
    tab = jnp.repeat(block_table.T, 32, axis=1)
    lanes = jnp.repeat(own_len, 32)
    meta = jnp.concatenate([(lanes // 64)[None], (lanes % 64)[None], jnp.zeros((6, HD), jnp.int32)])
    pdest = lax.dynamic_slice_in_dim(dests, inst * 48 + (tp // 2) * 24, 24)
    order = jnp.arange(24, dtype=jnp.int32)
    match = pdest[None, :] == jnp.arange(64, dtype=jnp.int32)[:, None]
    first = jnp.min(jnp.where(match, order, 24), axis=1)
    last = jnp.max(jnp.where(match, order, -1), axis=1)
    index = jnp.stack([first, jnp.where(last > first, last, 24)])

    smem = pl.BlockSpec(memory_space=pltpu.SMEM)
    vmem = pl.BlockSpec(memory_space=pltpu.VMEM)
    hbm = pl.BlockSpec(memory_space=pl.ANY)
    sem = lambda *shape: pltpu.SemaphoreType.DMA(shape)
    V = pltpu.VMEM
    return pl.pallas_call(
        body,
        out_shape=jax.ShapeDtypeStruct((5, 4, 16, HD), BF16),
        in_specs=[smem, smem, smem, vmem, vmem, vmem, hbm, hbm],
        out_specs=vmem,
        scratch_shapes=[
            V((48, 2, 2, 64, HD), BF16),
            V((2, 2, 12, 2, 2, 64, HD), BF16),
            V((12, 8, HD), F32),
            V((80, HD), BF16),
            V((3, 80, HD), BF16),
            V((4, 4, 16, HD), BF16),
            V((4, 16, HD), BF16),
            V((3, 4, 16, HD), BF16),
            V((4, 4, 8, 32, HD), BF16),
            V((4, 4, 8, 32, HD), BF16),
            V((25, HD, HD), F32),
            V((25, 1, HD), F32),
            V((4, 16, 64, HD), BF16),
            V((4, 16, 64, HD), BF16),
            V((4, 16, HD), F32),
            V((4, 16, HD), F32),
            V((3, 16, 64, HD), BF16),
            V((3, 16, 64, HD), BF16),
            V((3, 16, HD), F32),
            V((3, 16, HD), F32),
            V((4, 4, 64, HD), BF16),
            V((4, 4, 64, HD), BF16),
            V((4, 8, HD), F32),
            V((4, 8, HD), F32),
            V((3, 4, 64, HD), BF16),
            V((3, 4, 64, HD), BF16),
            V((3, 8, HD), F32),
            V((3, 8, HD), F32),
            V((4, HD, HD), BF16),
            V((4, 8, HD), F32),
            V((7, HD, HD), BF16),
            V((7, 8, HD), F32),
            V((4, 16, HD), F32),
            V((HD, HD), F32),
            sem(3), sem(2), sem(2), sem(3), sem(3), sem(3), sem(3),
            sem(2, 7), sem(2, 7), sem(2, 3), sem(2, 3), sem(2, 3), sem(2, 3),
            sem(4, 3), sem(4, 3), sem(4, 3), sem(4, 3), sem(2, 7), sem(2, 7),
        ],
        compiler_params=pltpu.CompilerParams(
            collective_id=0, has_side_effects=True, vmem_limit_bytes=48 * 1024 * 1024
        ),
    )(scal, pdest, index, tab, meta, pack, pool_kv, prompt_kv)


def solution(mesh):
    placed = (
        P("inst", None, "tp", None, None),
        P("inst", None),
        P(),
        P(),
        P(),
        P(("inst", "tp"), None, None, None, None),
        P(),
        P("inst", None, "tp", None),
        P("inst", None, None, "tp", None),
    )
    return jax.shard_map(
        per_device,
        mesh=mesh,
        in_specs=placed,
        out_specs=P("inst", None, "tp", None),
        check_vma=False,
    )
```

```python
import math

import jax
import jax.numpy as jnp
import numpy as np
from jax import lax
from jax.experimental import pallas as pl
from jax.experimental.pallas import tpu as pltpu
from jax.sharding import PartitionSpec as P

MESH = pl.DeviceIdType.MESH
NEG = -1e30
F32 = jnp.float32
BF16 = jnp.bfloat16
HD = 128
SCALE = 1.0 / math.sqrt(HD)
UNROLL = 3


def rope_row():
    ratio = np.arange(HD // 2) * (2.0 / HD)
    base = np.exp(-ratio * math.log(500000.0))
    wavelength = 2.0 * math.pi / base
    smooth = (8192.0 / wavelength - 1.0) / 3.0
    blended = (1.0 - smooth) * base / 8.0 + smooth * base
    freqs = np.where(wavelength < 2048.0, base, np.where(wavelength > 8192.0, base / 8.0, blended))
    return np.concatenate([freqs, freqs])[None].astype(np.float32)


def cos_sin(angle):
    turns = jnp.floor(angle * (2.0 / math.pi) + 0.5)
    r = angle - turns * 1.5703125
    r = r - turns * 4.837512969970703125e-4
    r = r - turns * 7.54978995489188216e-8
    sq = r * r
    sine = ((-1.9515295891e-4 * sq + 8.3321608736e-3) * sq - 1.6666654611e-1) * sq * r + r
    cosine = (2.443315711809948e-5 * sq - 1.388731625493765e-3) * sq + 4.166664568298827e-2
    cosine = cosine * sq * sq - 0.5 * sq + 1.0
    quarter = turns - 4.0 * jnp.floor(turns * 0.25)
    odd = (quarter == 1.0) | (quarter == 3.0)
    first, second = jnp.where(odd, sine, cosine), jnp.where(odd, cosine, sine)
    first = jnp.where((quarter == 1.0) | (quarter == 2.0), -first, first)
    second = jnp.where(quarter >= 2.0, -second, second)
    return first, second


def dot_nt(a, b):
    return lax.dot_general(a, b, (((1,), (1,)), ((), ())), preferred_element_type=F32)


def dot_tn(a, b):
    return lax.dot_general(a, b, (((0,), (0,)), ((), ())), preferred_element_type=F32)


def shares(parts):
    top = parts[0]
    for part in parts[1:]:
        top = jnp.maximum(top, part)
    weights = [jnp.exp(part - top) for part in parts]
    total = weights[0]
    for part in weights[1:]:
        total = total + part
    return [part / total for part in weights], top + jnp.log(total)


def iota(shape, axis):
    return lax.broadcasted_iota(jnp.int32, shape, axis)


def body(
    dests, lengths, partner, mig_slot, table, dest_grid, freqs, queries, step_kv, pool_hbm, prompt_hbm, out,
    pool, pages, ab, index_v, index, mig_mine, mig_send, mig_rcv, ret_loc, ret_send, ret_rcv,
    zqa, zqb, qa_low, qa_high, qb_low, qb_high, acc, lse, acc2, lse2,
    sa, sb, la, lb, ra, rb, rla, rlb,
    sa2, sb2, la2, lb2, ra2, rb2, rla2, rlb2,
    s3, l3, r3, rl3,
    local_sem, core_ssem, core_rsem, mig_ssem, mig_rsem, ret_ssem, ret_rsem,
    gz_ssem, gz_rsem, g2_ssem, g2_rsem, g3_ssem, g3_rsem,
    r1_ssem, r1_rsem, r2_ssem, r2_rsem, rz_ssem, rz_rsem,
):
    inst = lax.axis_index("inst")
    tp = lax.axis_index("tp")
    z_lo, y, x = inst // 16, (inst // 4) % 4, inst % 4
    z_hi, core = tp // 2, tp % 2
    z = z_hi * 4 + z_lo

    def device(zz, yy, xx, cc):
        return ((zz % 4) * 16 + yy * 4 + xx, (zz // 4) * 2 + cc)

    x_peers = [device(z, y, (x + k) % 4, core) for k in (1, 2, 3)]
    y_peers = [device(z, (y + k) % 4, x, core) for k in (1, 2, 3)]
    z_peers = [device((z + k) % 8, y, x, core) for k in range(1, 8)]
    core_peer = device(z, y, x, 1 - core)
    mig_peers = [
        device(z, y, x + 1 - 2 * (x % 2), core),
        device(z, y, (x + 2) % 4, core),
        device(z, y + 1 - 2 * (y % 2), x, core),
    ]

    barrier = pltpu.get_barrier_semaphore()
    everyone = [core_peer] + x_peers + y_peers + z_peers
    for peer in everyone:
        pl.semaphore_signal(barrier, inc=1, device_id=peer, device_id_type=MESH)

    def remote(src, dst, ssem, rsem, peer):
        return pltpu.make_async_remote_copy(
            src_ref=src, dst_ref=dst, send_sem=ssem, recv_sem=rsem,
            device_id=peer, device_id_type=MESH,
        )

    pool_copy = pltpu.make_async_copy(pool_hbm, pool, local_sem.at[0])
    pool_copy.start()
    own_copies = [
        pltpu.make_async_copy(
            prompt_hbm.at[:, :, pl.ds(hi * 4 + core * 2, 2)], pages.at[core, hi], local_sem.at[1 + hi]
        )
        for hi in range(2)
    ]
    for copy in own_copies:
        copy.start()

    my_slot = mig_slot[inst]
    mate = partner[inst]
    mate_len = lengths[mig_slot[mate], mate]
    own_len = [lengths[j, inst] for j in range(4)]
    bit = jnp.where(mate // 4 != inst // 4, 2, jnp.where(mate // 2 != inst // 2, 1, 0))
    first_row = inst * 48 + z_hi * 24

    freq = freqs[...]
    lane8 = iota((8, HD), 1)
    line8 = iota((8, HD), 0)
    line16 = iota((16, HD), 0)
    sign = jnp.where(lane8[:1] < 64, -1.0, 1.0)
    is_key = (line16 // 2) % 2 == 0

    def tables(length):
        at = length + (line8 % 4).astype(F32)
        cosine, sine = cos_sin(at * freq)
        return cosine, sine * sign

    def key_tables(length):
        at = jnp.where(is_key, length + (line16 // 4).astype(F32), 0.0)
        cosine, sine = cos_sin(at * freq)
        return cosine, sine * sign

    def turn(value, cosine, sine):
        return value * cosine + pltpu.roll(value, 64, 1) * sine

    def turned_query(slot, cosine, sine):
        tiles = [[None] * 4, [None] * 4]
        for s in range(4):
            both = queries[slot, s].astype(F32)
            for h in range(2):
                tiles[h][s] = turn(both[h * 8 : h * 8 + 8], cosine[s : s + 1], sine[s : s + 1])
        return [jnp.concatenate(part, axis=0).astype(BF16) for part in tiles]

    named_here = jnp.where(dest_grid[...] == inst, 1.0, 0.0)
    new_len = jnp.sum(jnp.sum(named_here, axis=0, keepdims=True), axis=1, keepdims=True) * 64.0
    mine = turned_query(4, *tables(new_len))
    zqa[z] = mine[0]
    zqb[z] = mine[1]
    qa, qb = (qa_low, qa_high), (qb_low, qb_high)

    pl.semaphore_wait(barrier, len(everyone))

    gz = []
    for k in range(7):
        here = zqa.at[z]
        gz.append(remote(here, here, gz_ssem.at[0, k], gz_rsem.at[0, k], z_peers[k]))
        here = zqb.at[z]
        gz.append(remote(here, here, gz_ssem.at[1, k], gz_rsem.at[1, k], z_peers[k]))
    for copy in gz:
        copy.start()

    for j in range(4):
        length = jnp.where(my_slot == j, mate_len, own_len[j]).astype(F32)
        part = turned_query(j, *tables(length))
        mig_mine[j, pl.ds(0, 32)] = part[0]
        mig_mine[j, pl.ds(32, 32)] = part[1]
        mig_mine[j, pl.ds(64, 16)] = turn(step_kv[j].astype(F32), *key_tables(length)).astype(BF16)
    mig_send[...] = mig_mine[my_slot]
    mig = [remote(mig_send, mig_rcv.at[k], mig_ssem.at[k], mig_rsem.at[k], mig_peers[k]) for k in range(3)]
    for copy in mig:
        copy.start()
    core_copies = [
        remote(
            prompt_hbm.at[:, :, pl.ds(hi * 4 + (1 - core) * 2, 2)],
            pages.at[core, hi], core_ssem.at[hi], core_rsem.at[hi], core_peer,
        )
        for hi in range(2)
    ]
    for copy in core_copies:
        copy.start()

    first = jnp.full((8, HD), 24, jnp.int32)
    second = jnp.full((8, HD), 24, jnp.int32)
    for n in range(24):
        hit = lane8 == dests[first_row + n]
        second = jnp.where(hit & (first < 24), n, second)
        first = jnp.where(hit & (first == 24), n, first)
    index_v[...] = jnp.where(line8 == 0, first, second)
    index_copy = pltpu.make_async_copy(index_v, index, local_sem.at[3])
    index_copy.start()

    twice = jnp.concatenate(mine + mine, axis=0)
    own_kv = turn(step_kv[4].astype(F32), *key_tables(new_len)).astype(BF16)
    lane16 = iota((16, HD), 1)
    ok = is_key & (line16 % 2 == (lane16 % 64) // 32) & (line16 // 4 <= (lane16 % 32) // 8)
    score = jnp.where(ok, dot_nt(own_kv, twice) * SCALE, NEG)
    top = jnp.max(score, axis=0, keepdims=True)
    weight = jnp.where(ok, jnp.exp(score - top), 0.0).astype(BF16).astype(F32)
    total = jnp.sum(weight, axis=0, keepdims=True)
    new_acc = dot_tn(own_kv, pltpu.roll(weight, 2, 0).astype(BF16)) / total
    new_acc = jnp.where(iota((64, HD), 1) < 64, new_acc[:64], new_acc[64:])
    new_lse = top + jnp.log(total)

    shape = (12, 8, HD)
    row = iota(shape, 1)
    page_id = iota(shape, 0) * 4 + row % 4
    is_last = row // 4
    lane1 = lane8[:1]

    def by_slot(values):
        return jnp.where(
            lane1 < 64, jnp.where(lane1 < 32, values[0], values[1]), jnp.where(lane1 < 96, values[2], values[3])
        )

    context = by_slot(own_len)
    full, rem = context // 64, context % 64
    ab[...] = jnp.zeros(shape, F32)

    def count_step(k, carry):
        named = by_slot([table[j, k] for j in range(4)])[None]
        kind = jnp.where(k < full, 0, jnp.where(k == full, 1, 2))[None]
        hit = (page_id == named) & (is_last == kind)
        ab[...] += jnp.where(hit, 1.0, 0.0)
        return carry

    lax.fori_loop(0, 24, count_step, 0)

    for copy in gz:
        copy.wait()
    g2 = []
    for hi in range(2):
        for k in range(3):
            here = zqa.at[pl.ds(hi * 4, 4)]
            g2.append(remote(here, qa[hi].at[x, y], g2_ssem.at[hi, 0, k], g2_rsem.at[hi, 0, k], y_peers[k]))
            here = zqb.at[pl.ds(hi * 4, 4)]
            g2.append(remote(here, qb[hi].at[y, x], g2_ssem.at[hi, 1, k], g2_rsem.at[hi, 1, k], x_peers[k]))
    for copy in g2:
        copy.start()
    for hi in range(2):
        qa[hi][x, y] = zqa[pl.ds(hi * 4, 4)]
        qb[hi][y, x] = zqb[pl.ds(hi * 4, 4)]
    for copy in mig:
        copy.wait()

    came = mig_rcv[bit].astype(F32)
    blocks = [jnp.where(my_slot == j, came, mig_mine[j].astype(F32)).astype(BF16) for j in range(4)]
    fresh_kv = jnp.concatenate([block[64:80] for block in blocks], axis=0)
    q_res = [jnp.concatenate([block[h * 32 : h * 32 + 32] for block in blocks], axis=0) for h in range(2)]
    pool_copy.wait()
    below = (iota((64, HD), 0) < rem).astype(F32)

    def res_step(i, carry):
        named = ab[i]
        count = (named[0:4][:, None, :] + named[4:8][:, None, :] * below[None]).reshape(256, HD)
        real = count > 0.0
        after = []
        for h in range(2):
            best, total, summed = carry[3 * h : 3 * h + 3]
            keys = pool[pl.ds(i * 4, 4), 0, h].reshape(256, HD)
            values = pool[pl.ds(i * 4, 4), 1, h].reshape(256, HD)
            score = jnp.where(real, dot_nt(keys, q_res[h]) * SCALE, NEG)
            top = jnp.maximum(best, jnp.max(score, axis=0, keepdims=True))
            weight = (count * jnp.exp(score - top)).astype(BF16)
            shrink = jnp.exp(best - top)
            total = total * shrink + jnp.sum(weight.astype(F32), axis=0, keepdims=True)
            summed = summed * shrink + dot_tn(values, weight)
            after += [top, total, summed]
        return tuple(after)

    start = (jnp.full((1, HD), NEG, F32), jnp.zeros((1, HD), F32), jnp.zeros((HD, HD), F32)) * 2
    state = lax.fori_loop(0, 4, res_step, start)
    for copy in g2:
        copy.wait()
    g3 = [[], []]
    for hi in range(2):
        for k in range(3):
            here = qa[hi].at[x]
            g3[hi].append(remote(here, here, g3_ssem.at[hi, 0, k], g3_rsem.at[hi, 0, k], x_peers[k]))
            here = qb[hi].at[y]
            g3[hi].append(remote(here, here, g3_ssem.at[hi, 1, k], g3_rsem.at[hi, 1, k], y_peers[k]))
        for copy in g3[hi]:
            copy.start()

    state = lax.fori_loop(4, 12, res_step, state)
    lane = iota((64, HD), 1)
    line = iota((64, HD), 0)
    ok_slot = (line // 16 == lane // 32) & ((line // 2) % 2 == 0) & ((line % 16) // 4 <= (lane % 32) // 8)
    rows = []
    for h in range(2):
        best, total, summed = state[3 * h : 3 * h + 3]
        ok = ok_slot & (line % 2 == h)
        score = jnp.where(ok, dot_nt(fresh_kv, q_res[h]) * SCALE, NEG)
        top = jnp.maximum(best, jnp.max(score, axis=0, keepdims=True))
        weight = jnp.where(ok, jnp.exp(score - top), 0.0).astype(BF16).astype(F32)
        shrink = jnp.exp(best - top)
        total = total * shrink + jnp.sum(weight, axis=0, keepdims=True)
        summed = summed * shrink + dot_tn(fresh_kv, pltpu.roll(weight, 2, 0).astype(BF16))
        rows.append((summed / total).T)
    for j in range(4):
        for s in range(4):
            at = j * 32 + s * 8
            ret_loc[j, s] = jnp.concatenate([rows[0][at : at + 8], rows[1][at : at + 8]], axis=0).astype(BF16)
    ret_send[...] = ret_loc[my_slot]
    ret = [remote(ret_send, ret_rcv.at[k], ret_ssem.at[k], ret_rsem.at[k], mig_peers[k]) for k in range(3)]
    for copy in ret:
        copy.start()

    for copy in own_copies + core_copies:
        copy.wait()
    index_copy.wait()
    acc[24] = jnp.zeros((HD, HD), F32)
    acc2[24] = jnp.zeros((HD, HD), F32)
    lse[24] = jnp.full((1, HD), NEG, F32)
    lse2[24] = jnp.full((1, HD), NEG, F32)
    same_head = iota((HD, HD), 0) // 64 == (iota((HD, HD), 1) % 64) // 32
    left = iota((HD, HD), 1) < 64
    left1 = lane1 < 64
    zeros6 = jnp.zeros((6, HD), F32)

    def prompt_part(hi):
        def page(n, src, i):
            d = dests[first_row + n]
            zl, dy, dx = d // 16, (d // 4) % 4, d % 4
            half = [qa[hi][dx, dy, zl], qb[hi][dy, dx, zl]]
            asked = jnp.concatenate(half + half, axis=0)
            score = jnp.where(same_head, dot_nt(pages[src, hi, i, 0].reshape(HD, HD), asked) * SCALE, NEG)
            top = jnp.max(score, axis=0, keepdims=True)
            weight = jnp.exp(score - top).astype(BF16)
            total = jnp.sum(weight.astype(F32), axis=0, keepdims=True)
            acc[n] = dot_tn(pages[src, hi, i, 1].reshape(HD, HD), weight) / total
            lse[n] = top + jnp.log(total)

        def page_step(i, carry):
            for src in range(2):
                for more in range(UNROLL):
                    page(src * 12 + i * UNROLL + more, src, i * UNROLL + more)
            return carry

        lax.fori_loop(0, 12 // UNROLL, page_step, 0)

        def join_step(i, carry):
            for more in range(4):
                n = i * 4 + more
                d = dests[first_row + n]
                first = index[0, d]
                other = jnp.where(first == n, index[1, d], first)
                weights, joined = shares([lse[n], lse[other]])
                acc2[n] = acc[n] * weights[0] + acc[other] * weights[1]
                lse2[n] = joined
            return carry

        lax.fori_loop(0, 6, join_step, 0)

        for zp in range(2):
            def place_step(dy, carry):
                for dx in range(4):
                    d = zp * 32 + dy * 4 + dx
                    one, two = index[0, d], index[0, d + 16]
                    block = jnp.where(left, acc2[one], acc2[two]).astype(BF16)
                    stat = jnp.where(left1, lse2[one], lse2[two])
                    sa[hi, dx, dy * 2 + zp] = block[:64]
                    sb[hi, dy, dx * 2 + zp] = block[64:]
                    la[hi, dx, pl.ds(dy * 2 + zp, 1), :] = stat
                    lb[hi, dy, pl.ds(dx * 2 + zp, 1), :] = stat
                return carry

            lax.fori_loop(0, 4, place_step, 0)

    def send_first(hi):
        sent = []
        for k in range(3):
            to_x, to_y = (x + k + 1) % 4, (y + k + 1) % 4
            for m, (src, dst, peer) in enumerate((
                (sa.at[hi, to_x], ra.at[hi, k], x_peers[k]),
                (sb.at[hi, to_y], rb.at[hi, k], y_peers[k]),
                (la.at[hi, to_x], rla.at[hi, k], x_peers[k]),
                (lb.at[hi, to_y], rlb.at[hi, k], y_peers[k]),
            )):
                sent.append(remote(src, dst, r1_ssem.at[hi, m, k], r1_rsem.at[hi, m, k], peer))
        for copy in sent:
            copy.start()
        return sent

    def merge_first(hi):
        for mine_s, mine_l, got_s, got_l, where, next_s, next_l in (
            (sa, la, ra, rla, x, sa2, la2), (sb, lb, rb, rlb, y, sb2, lb2)
        ):
            weights, joined = shares([mine_l[hi, where]] + [got_l[hi, k] for k in range(3)])
            for t in range(8):
                block = mine_s[hi, where, t].astype(F32) * weights[0][t : t + 1]
                for k in range(3):
                    block = block + got_s[hi, k, t].astype(F32) * weights[k + 1][t : t + 1]
                next_s[hi, t // 2, t % 2] = block.astype(BF16)
            for group in range(4):
                next_l[hi, group] = jnp.concatenate([joined[group * 2 : group * 2 + 2], zeros6], axis=0)

    def send_second(hi):
        sent = []
        for k in range(3):
            to_x, to_y = (x + k + 1) % 4, (y + k + 1) % 4
            for m, (src, dst, peer) in enumerate((
                (sa2.at[hi, to_y], ra2.at[hi, k], y_peers[k]),
                (sb2.at[hi, to_x], rb2.at[hi, k], x_peers[k]),
                (la2.at[hi, to_y], rla2.at[hi, k], y_peers[k]),
                (lb2.at[hi, to_x], rlb2.at[hi, k], x_peers[k]),
            )):
                sent.append(remote(src, dst, r2_ssem.at[hi, m, k], r2_rsem.at[hi, m, k], peer))
        for copy in sent:
            copy.start()
        return sent

    left64 = lane < 64

    def merge_second(hi):
        sides = []
        for mine_s, mine_l, got_s, got_l, where in ((sa2, la2, ra2, rla2, y), (sb2, lb2, rb2, rlb2, x)):
            weights, joined = shares([mine_l[hi, where]] + [got_l[hi, k] for k in range(3)])
            blocks = []
            for zp in range(2):
                block = mine_s[hi, where, zp].astype(F32) * weights[0][zp : zp + 1]
                for k in range(3):
                    block = block + got_s[hi, k, zp].astype(F32) * weights[k + 1][zp : zp + 1]
                blocks.append(block)
            sides.append((blocks, joined))
        for zp in range(2):
            a, b = sides[0][0][zp], sides[1][0][zp]
            s3[hi * 4 + zp * 2] = jnp.where(left64, a, pltpu.roll(b, 64, 1)).astype(BF16)
            s3[hi * 4 + zp * 2 + 1] = jnp.where(left64, pltpu.roll(a, 64, 1), b).astype(BF16)
            a, b = sides[0][1], sides[1][1]
            l3[hi * 4 + zp * 2] = jnp.where(lane8 < 64, a, pltpu.roll(b, 64, 1))[zp : zp + 1]
            l3[hi * 4 + zp * 2 + 1] = jnp.where(lane8 < 64, pltpu.roll(a, 64, 1), b)[zp : zp + 1]

    for copy in g3[0]:
        copy.wait()
    prompt_part(0)
    r1_low = send_first(0)
    for copy in g3[1]:
        copy.wait()
    prompt_part(1)
    r1_high = send_first(1)
    for copy in ret:
        copy.wait()
    back = [ret_rcv[bit, s].astype(F32) for s in range(4)]
    for j in range(4):
        for s in range(4):
            out[j, s] = jnp.where(my_slot == j, back[s], ret_loc[j, s].astype(F32)).astype(BF16)
    for copy in r1_low:
        copy.wait()
    merge_first(0)
    r2_low = send_second(0)
    for copy in r1_high:
        copy.wait()
    merge_first(1)
    r2_high = send_second(1)
    for copy in r2_low:
        copy.wait()
    merge_second(0)
    for copy in r2_high:
        copy.wait()
    merge_second(1)

    rz = []
    for k in range(7):
        to = (z + k + 1) % 8
        rz.append(remote(s3.at[to], r3.at[k], rz_ssem.at[0, k], rz_rsem.at[0, k], z_peers[k]))
        rz.append(remote(l3.at[to], rl3.at[k], rz_ssem.at[1, k], rz_rsem.at[1, k], z_peers[k]))
    for copy in rz:
        copy.start()
    for copy in rz:
        copy.wait()
    weights, _ = shares([new_lse, l3[z]] + [rl3[k] for k in range(7)])
    block = new_acc * weights[0] + s3[z].astype(F32) * weights[1]
    for k in range(7):
        block = block + r3[k].astype(F32) * weights[k + 2]
    flat = jnp.concatenate([block, block], axis=0).T
    here = jnp.where(left64, flat[:64], flat[64:])
    for s in range(4):
        out[4, s] = jnp.concatenate([here[s * 8 : s * 8 + 8], here[32 + s * 8 : 40 + s * 8]], axis=0).astype(BF16)


def per_device(
    pool_kv, block_table, context_len, partner, mig_slot, prompt_kv, prompt_dest, queries, step_kv
):
    smem = pl.BlockSpec(memory_space=pltpu.SMEM)
    vmem = pl.BlockSpec(memory_space=pltpu.VMEM)
    hbm = pl.BlockSpec(memory_space=pltpu.HBM)
    sem = lambda *shape: pltpu.SemaphoreType.DMA(shape)
    V = pltpu.VMEM
    return pl.pallas_call(
        body,
        out_shape=jax.ShapeDtypeStruct((5, 4, 16, HD), BF16),
        in_specs=[smem] * 5 + [vmem] * 4 + [hbm] * 2,
        out_specs=vmem,
        scratch_shapes=[
            V((48, 2, 2, 64, HD), BF16),
            V((2, 2, 12, 2, 2, 64, HD), BF16),
            V((12, 8, HD), F32),
            V((8, HD), jnp.int32),
            pltpu.SMEM((8, HD), jnp.int32),
            V((4, 80, HD), BF16),
            V((80, HD), BF16),
            V((3, 80, HD), BF16),
            V((4, 4, 16, HD), BF16),
            V((4, 16, HD), BF16),
            V((3, 4, 16, HD), BF16),
            V((8, 32, HD), BF16),
            V((8, 32, HD), BF16),
            V((4, 4, 4, 32, HD), BF16),
            V((4, 4, 4, 32, HD), BF16),
            V((4, 4, 4, 32, HD), BF16),
            V((4, 4, 4, 32, HD), BF16),
            V((25, HD, HD), F32),
            V((25, 1, HD), F32),
            V((25, HD, HD), F32),
            V((25, 1, HD), F32),
            V((2, 4, 8, 64, HD), BF16),
            V((2, 4, 8, 64, HD), BF16),
            V((2, 4, 8, HD), F32),
            V((2, 4, 8, HD), F32),
            V((2, 3, 8, 64, HD), BF16),
            V((2, 3, 8, 64, HD), BF16),
            V((2, 3, 8, HD), F32),
            V((2, 3, 8, HD), F32),
            V((2, 4, 2, 64, HD), BF16),
            V((2, 4, 2, 64, HD), BF16),
            V((2, 4, 8, HD), F32),
            V((2, 4, 8, HD), F32),
            V((2, 3, 2, 64, HD), BF16),
            V((2, 3, 2, 64, HD), BF16),
            V((2, 3, 8, HD), F32),
            V((2, 3, 8, HD), F32),
            V((8, 64, HD), BF16),
            V((8, 1, HD), F32),
            V((7, 64, HD), BF16),
            V((7, 1, HD), F32),
            sem(4), sem(2), sem(2), sem(3), sem(3), sem(3), sem(3),
            sem(2, 7), sem(2, 7), sem(2, 2, 3), sem(2, 2, 3), sem(2, 2, 3), sem(2, 2, 3),
            sem(2, 4, 3), sem(2, 4, 3), sem(2, 4, 3), sem(2, 4, 3), sem(2, 7), sem(2, 7),
        ],
        compiler_params=pltpu.CompilerParams(
            collective_id=0, has_side_effects=True, vmem_limit_bytes=60 * 1024 * 1024
        ),
    )(
        prompt_dest.reshape(-1), context_len.T, partner, mig_slot, block_table,
        prompt_dest.reshape(24, HD), jnp.asarray(rope_row()), queries, step_kv.reshape(5, 16, HD),
        pool_kv, prompt_kv,
    )


def solution(mesh):
    placed = (
        P("inst", None, "tp", None, None),
        P("inst", None),
        P(),
        P(),
        P(),
        P(("inst", "tp"), None, None, None, None),
        P(),
        P("inst", None, "tp", None),
        P("inst", None, None, "tp", None),
    )
    return jax.shard_map(
        per_device,
        mesh=mesh,
        in_specs=placed,
        out_specs=P("inst", None, "tp", None),
        check_vma=False,
    )
```

```python
import math

import jax
import jax.numpy as jnp
import numpy as np
from jax import lax
from jax.experimental import pallas as pl
from jax.experimental.pallas import tpu as pltpu
from jax.sharding import PartitionSpec as P

MESH = pl.DeviceIdType.MESH
NEG = -1e30
F32 = jnp.float32
BF16 = jnp.bfloat16
HD = 128
SCALE = 1.0 / math.sqrt(HD)
UNROLL = 3


def rope_row():
    ratio = np.arange(HD // 2) * (2.0 / HD)
    base = np.exp(-ratio * math.log(500000.0))
    wavelength = 2.0 * math.pi / base
    smooth = (8192.0 / wavelength - 1.0) / 3.0
    blended = (1.0 - smooth) * base / 8.0 + smooth * base
    freqs = np.where(wavelength < 2048.0, base, np.where(wavelength > 8192.0, base / 8.0, blended))
    return np.concatenate([freqs, freqs])[None].astype(np.float32)


def cos_sin(angle):
    turns = jnp.floor(angle * (2.0 / math.pi) + 0.5)
    r = angle - turns * 1.5703125
    r = r - turns * 4.837512969970703125e-4
    r = r - turns * 7.54978995489188216e-8
    sq = r * r
    sine = ((-1.9515295891e-4 * sq + 8.3321608736e-3) * sq - 1.6666654611e-1) * sq * r + r
    cosine = (2.443315711809948e-5 * sq - 1.388731625493765e-3) * sq + 4.166664568298827e-2
    cosine = cosine * sq * sq - 0.5 * sq + 1.0
    quarter = turns - 4.0 * jnp.floor(turns * 0.25)
    odd = (quarter == 1.0) | (quarter == 3.0)
    first, second = jnp.where(odd, sine, cosine), jnp.where(odd, cosine, sine)
    first = jnp.where((quarter == 1.0) | (quarter == 2.0), -first, first)
    second = jnp.where(quarter >= 2.0, -second, second)
    return first, second


def dot_nn(a, b):
    return lax.dot_general(a, b, (((1,), (0,)), ((), ())), preferred_element_type=F32)


def dot_tn(a, b):
    return lax.dot_general(a, b, (((0,), (0,)), ((), ())), preferred_element_type=F32)


def shares(parts):
    top = parts[0]
    for part in parts[1:]:
        top = jnp.maximum(top, part)
    weights = [jnp.exp(part - top) for part in parts]
    total = weights[0]
    for part in weights[1:]:
        total = total + part
    return [part / total for part in weights], top + jnp.log(total)


def iota(shape, axis):
    return lax.broadcasted_iota(jnp.int32, shape, axis)


def body(
    dests_in, lengths_in, partner_in, mig_slot_in, table_in, grid_in, freqs_in, queries_in, kv_in,
    pool_hbm, prompt_hbm, out,
    dests, lengths, partner, mig_slot, table, dest_grid, freqs, queries, step_kv,
    pool, pages, ab, index_v, index, mig_mine, mig_send, mig_rcv, ret_loc, ret_send, ret_rcv,
    zq, qa_low, qa_high, qb_low, qb_high, acc, lse, acc2, lse2,
    sa, sb, la, lb, ra, rb, rla, rlb,
    sa2, sb2, la2, lb2, ra2, rb2, rla2, rlb2,
    s3, l3, r3, rl3,
    in_sem, local_sem, core_ssem, core_rsem, mig_ssem, mig_rsem, ret_ssem, ret_rsem,
    gz_ssem, gz_rsem, g2_ssem, g2_rsem, g3_ssem, g3_rsem,
    r1_ssem, r1_rsem, r2_ssem, r2_rsem, rz_ssem, rz_rsem,
):
    inst = lax.axis_index("inst")
    tp = lax.axis_index("tp")
    z_lo, y, x = inst // 16, (inst // 4) % 4, inst % 4
    z_hi, core = tp // 2, tp % 2
    z = z_hi * 4 + z_lo

    def device(zz, yy, xx, cc):
        return ((zz % 4) * 16 + yy * 4 + xx, (zz // 4) * 2 + cc)

    x_peers = [device(z, y, (x + k) % 4, core) for k in (1, 2, 3)]
    y_peers = [device(z, (y + k) % 4, x, core) for k in (1, 2, 3)]
    z_peers = [device((z + k) % 8, y, x, core) for k in range(1, 8)]
    core_peer = device(z, y, x, 1 - core)
    mig_peers = [
        device(z, y, x + 1 - 2 * (x % 2), core),
        device(z, y, (x + 2) % 4, core),
        device(z, y + 1 - 2 * (y % 2), x, core),
    ]

    barrier = pltpu.get_barrier_semaphore()
    everyone = [core_peer] + x_peers + y_peers + z_peers
    for peer in everyone:
        pl.semaphore_signal(barrier, inc=1, device_id=peer, device_id_type=MESH)

    def remote(src, dst, ssem, rsem, peer):
        return pltpu.make_async_remote_copy(
            src_ref=src, dst_ref=dst, send_sem=ssem, recv_sem=rsem,
            device_id=peer, device_id_type=MESH,
        )

    inputs = [
        pltpu.make_async_copy(src, dst, in_sem.at[n])
        for n, (src, dst) in enumerate((
            (grid_in, dest_grid), (freqs_in, freqs), (queries_in, queries), (mig_slot_in, mig_slot),
            (partner_in, partner), (lengths_in, lengths), (dests_in, dests), (table_in, table), (kv_in, step_kv),
        ))
    ]
    for copy in inputs:
        copy.start()
    pool_copy = pltpu.make_async_copy(pool_hbm, pool, local_sem.at[0])
    pool_copy.start()
    own_copies = [
        pltpu.make_async_copy(
            prompt_hbm.at[:, :, pl.ds(hi * 4 + core * 2, 2)], pages.at[core, hi], local_sem.at[1 + hi]
        )
        for hi in range(2)
    ]
    for copy in own_copies:
        copy.start()

    first_row = inst * 48 + z_hi * 24

    for copy in inputs[:3]:
        copy.wait()
    freq = freqs[...]
    lane8 = iota((8, HD), 1)
    line8 = iota((8, HD), 0)
    line16 = iota((16, HD), 0)
    sign = jnp.where(lane8[:1] < 64, -1.0, 1.0)
    is_key = (line16 // 2) % 2 == 0

    def tables(length):
        at = length + (line8 % 4).astype(F32)
        cosine, sine = cos_sin(at * freq)
        return cosine, sine * sign

    def key_tables(length):
        at = jnp.where(is_key, length + (line16 // 4).astype(F32), 0.0)
        cosine, sine = cos_sin(at * freq)
        return cosine, sine * sign

    def turn(value, cosine, sine):
        return value * cosine + pltpu.roll(value, 64, 1) * sine

    def turned_query(slot, cosine, sine):
        tiles = [[None] * 4, [None] * 4]
        for s in range(4):
            both = queries[slot, s].astype(F32)
            for h in range(2):
                tiles[h][s] = turn(both[h * 8 : h * 8 + 8], cosine[s : s + 1], sine[s : s + 1])
        return [jnp.concatenate(part, axis=0) for part in tiles]

    named_here = jnp.where(dest_grid[...] == inst, 1.0, 0.0)
    new_len = jnp.sum(jnp.sum(named_here, axis=0, keepdims=True), axis=1, keepdims=True) * 64.0
    mine = turned_query(4, *tables(new_len))
    twice = jnp.concatenate(mine + mine, axis=0).T
    zq[z] = jnp.where(iota((64, HD), 1) < 64, twice[:64], twice[64:]).astype(BF16)
    twice = twice.astype(BF16)
    qa, qb = (qa_low, qa_high), (qb_low, qb_high)

    pl.semaphore_wait(barrier, len(everyone))

    gz = []
    for k in range(7):
        gz.append(remote(zq.at[z], zq.at[z], gz_ssem.at[k], gz_rsem.at[k], z_peers[k]))
    for copy in gz:
        copy.start()
    for copy in inputs[3:]:
        copy.wait()

    my_slot = mig_slot[inst]
    mate = partner[inst]
    mate_len = lengths[mig_slot[mate], mate]
    own_len = [lengths[j, inst] for j in range(4)]
    bit = jnp.where(mate // 4 != inst // 4, 2, jnp.where(mate // 2 != inst // 2, 1, 0))

    for j in range(4):
        length = jnp.where(my_slot == j, mate_len, own_len[j]).astype(F32)
        part = turned_query(j, *tables(length))
        mig_mine[j, pl.ds(0, 32)] = part[0].astype(BF16)
        mig_mine[j, pl.ds(32, 32)] = part[1].astype(BF16)
        mig_mine[j, pl.ds(64, 16)] = turn(step_kv[j].astype(F32), *key_tables(length)).astype(BF16)
    mig_send[...] = mig_mine[my_slot]
    mig = [remote(mig_send, mig_rcv.at[k], mig_ssem.at[k], mig_rsem.at[k], mig_peers[k]) for k in range(3)]
    for copy in mig:
        copy.start()
    core_copies = [
        remote(
            prompt_hbm.at[:, :, pl.ds(hi * 4 + (1 - core) * 2, 2)],
            pages.at[core, hi], core_ssem.at[hi], core_rsem.at[hi], core_peer,
        )
        for hi in range(2)
    ]
    for copy in core_copies:
        copy.start()

    first = jnp.full((8, HD), 24, jnp.int32)
    second = jnp.full((8, HD), 24, jnp.int32)
    for n in range(24):
        hit = lane8 == dests[first_row + n]
        second = jnp.where(hit & (first < 24), n, second)
        first = jnp.where(hit & (first == 24), n, first)
    index_v[...] = jnp.where(line8 == 0, first, second)
    index_copy = pltpu.make_async_copy(index_v, index, local_sem.at[3])
    index_copy.start()

    own_kv = turn(step_kv[4].astype(F32), *key_tables(new_len)).astype(BF16)
    lane16 = iota((16, HD), 1)
    ok = is_key & (line16 % 2 == (lane16 % 64) // 32) & (line16 // 4 <= (lane16 % 32) // 8)
    score = jnp.where(ok, dot_nn(own_kv, twice) * SCALE, NEG)
    top = jnp.max(score, axis=0, keepdims=True)
    weight = jnp.where(ok, jnp.exp(score - top), 0.0).astype(BF16).astype(F32)
    total = jnp.sum(weight, axis=0, keepdims=True)
    new_acc = dot_tn(own_kv, pltpu.roll(weight, 2, 0).astype(BF16)) / total
    new_acc = jnp.where(iota((64, HD), 1) < 64, new_acc[:64], new_acc[64:])
    new_lse = top + jnp.log(total)

    shape = (12, 8, HD)
    row = iota(shape, 1)
    page_id = iota(shape, 0) * 4 + row % 4
    is_last = row // 4
    lane1 = lane8[:1]

    def by_slot(values):
        return jnp.where(
            lane1 < 64, jnp.where(lane1 < 32, values[0], values[1]), jnp.where(lane1 < 96, values[2], values[3])
        )

    context = by_slot(own_len)
    full, rem = context // 64, context % 64
    ab[...] = jnp.zeros(shape, F32)

    def count_step(k, carry):
        named = by_slot([table[j, k] for j in range(4)])[None]
        kind = jnp.where(k < full, 0, jnp.where(k == full, 1, 2))[None]
        hit = (page_id == named) & (is_last == kind)
        ab[...] += jnp.where(hit, 1.0, 0.0)
        return carry

    lax.fori_loop(0, 24, count_step, 0)

    for copy in gz:
        copy.wait_recv()
    g2 = [[], []]
    for hi in range(2):
        part = zq.at[pl.ds(hi * 4, 4), pl.ds(0, 32)]
        other = zq.at[pl.ds(hi * 4, 4), pl.ds(32, 32)]
        for k in range(3):
            g2[hi].append(remote(part, qa[hi].at[x, y], g2_ssem.at[hi, 0, k], g2_rsem.at[hi, 0, k], y_peers[k]))
            g2[hi].append(remote(other, qb[hi].at[y, x], g2_ssem.at[hi, 1, k], g2_rsem.at[hi, 1, k], x_peers[k]))
        for copy in g2[hi]:
            copy.start()
    for hi in range(2):
        qa[hi][x, y] = zq[pl.ds(hi * 4, 4), pl.ds(0, 32)]
        qb[hi][y, x] = zq[pl.ds(hi * 4, 4), pl.ds(32, 32)]
    for copy in mig:
        copy.wait_recv()

    came = mig_rcv[bit].astype(F32)
    blocks = [jnp.where(my_slot == j, came, mig_mine[j].astype(F32)) for j in range(4)]
    fresh_kv = jnp.concatenate([block[64:80] for block in blocks], axis=0).astype(BF16)
    q_res = [
        jnp.concatenate([block[h * 32 : h * 32 + 32] for block in blocks], axis=0).T.astype(BF16) for h in range(2)
    ]
    pool_copy.wait()
    below = (iota((64, HD), 0) < rem).astype(F32)

    def res_step(i, carry):
        named = ab[i]
        count = (named[0:4][:, None, :] + named[4:8][:, None, :] * below[None]).reshape(256, HD)
        real = count > 0.0
        after = []
        for h in range(2):
            best, total, summed = carry[3 * h : 3 * h + 3]
            keys = pool[pl.ds(i * 4, 4), 0, h].reshape(256, HD)
            values = pool[pl.ds(i * 4, 4), 1, h].reshape(256, HD)
            score = jnp.where(real, dot_nn(keys, q_res[h]) * SCALE, NEG)
            top = jnp.maximum(best, jnp.max(score, axis=0, keepdims=True))
            weight = (count * jnp.exp(score - top)).astype(BF16)
            shrink = jnp.exp(best - top)
            total = total * shrink + jnp.sum(weight.astype(F32), axis=0, keepdims=True)
            summed = summed * shrink + dot_tn(values, weight)
            after += [top, total, summed]
        return tuple(after)

    start = (jnp.full((1, HD), NEG, F32), jnp.zeros((1, HD), F32), jnp.zeros((HD, HD), F32)) * 2
    state = lax.fori_loop(0, 4, res_step, start)
    g3 = [[], []]
    for hi in range(2):
        for copy in g2[hi]:
            copy.wait_recv()
        for k in range(3):
            here = qa[hi].at[x]
            g3[hi].append(remote(here, here, g3_ssem.at[hi, 0, k], g3_rsem.at[hi, 0, k], x_peers[k]))
            here = qb[hi].at[y]
            g3[hi].append(remote(here, here, g3_ssem.at[hi, 1, k], g3_rsem.at[hi, 1, k], y_peers[k]))
        for copy in g3[hi]:
            copy.start()

    state = lax.fori_loop(4, 12, res_step, state)
    lane = iota((64, HD), 1)
    line = iota((64, HD), 0)
    ok_slot = (line // 16 == lane // 32) & ((line // 2) % 2 == 0) & ((line % 16) // 4 <= (lane % 32) // 8)
    rows = []
    for h in range(2):
        best, total, summed = state[3 * h : 3 * h + 3]
        ok = ok_slot & (line % 2 == h)
        score = jnp.where(ok, dot_nn(fresh_kv, q_res[h]) * SCALE, NEG)
        top = jnp.maximum(best, jnp.max(score, axis=0, keepdims=True))
        weight = jnp.where(ok, jnp.exp(score - top), 0.0).astype(BF16).astype(F32)
        shrink = jnp.exp(best - top)
        total = total * shrink + jnp.sum(weight, axis=0, keepdims=True)
        summed = summed * shrink + dot_tn(fresh_kv, pltpu.roll(weight, 2, 0).astype(BF16))
        rows.append((summed / total).T)
    for j in range(4):
        for s in range(4):
            at = j * 32 + s * 8
            ret_loc[j, s] = jnp.concatenate([rows[0][at : at + 8], rows[1][at : at + 8]], axis=0).astype(BF16)
    ret_send[...] = ret_loc[my_slot]
    ret = [remote(ret_send, ret_rcv.at[k], ret_ssem.at[k], ret_rsem.at[k], mig_peers[k]) for k in range(3)]
    for copy in ret:
        copy.start()

    for copy in own_copies:
        copy.wait()
    for copy in core_copies:
        copy.wait_recv()
    index_copy.wait()
    acc[24] = jnp.zeros((HD, HD), F32)
    acc2[24] = jnp.zeros((HD, HD), F32)
    lse[24] = jnp.full((1, HD), NEG, F32)
    lse2[24] = jnp.full((1, HD), NEG, F32)
    same_head = iota((HD, HD), 0) // 64 == (iota((HD, HD), 1) % 64) // 32
    left = iota((HD, HD), 1) < 64
    left1 = lane1 < 64
    left64 = lane < 64
    zeros6 = jnp.zeros((6, HD), F32)

    def prompt_part(hi):
        def page(n, src, i):
            d = dests[first_row + n]
            zl, dy, dx = d // 16, (d // 4) % 4, d % 4
            part = jnp.concatenate([qa[hi][dx, dy, zl], qb[hi][dy, dx, zl]], axis=0)
            swap = jnp.concatenate([part[:, 64:], part[:, :64]], axis=1)
            asked = jnp.concatenate([jnp.where(left64, part, swap), jnp.where(left64, swap, part)], axis=0)
            score = jnp.where(same_head, dot_nn(pages[src, hi, i, 0].reshape(HD, HD), asked) * SCALE, NEG)
            top = jnp.max(score, axis=0, keepdims=True)
            weight = jnp.exp(score - top).astype(BF16)
            total = jnp.sum(weight.astype(F32), axis=0, keepdims=True)
            acc[n] = dot_tn(pages[src, hi, i, 1].reshape(HD, HD), weight) / total
            lse[n] = top + jnp.log(total)

        def page_step(i, carry):
            for src in range(2):
                for more in range(UNROLL):
                    page(src * 12 + i * UNROLL + more, src, i * UNROLL + more)
            return carry

        lax.fori_loop(0, 12 // UNROLL, page_step, 0)

        def join_step(i, carry):
            for more in range(4):
                n = i * 4 + more
                d = dests[first_row + n]
                first = index[0, d]
                other = jnp.where(first == n, index[1, d], first)
                weights, joined = shares([lse[n], lse[other]])
                acc2[n] = acc[n] * weights[0] + acc[other] * weights[1]
                lse2[n] = joined
            return carry

        lax.fori_loop(0, 6, join_step, 0)

        for zp in range(2):
            def place_step(dy, carry):
                for dx in range(4):
                    d = zp * 32 + dy * 4 + dx
                    one, two = index[0, d], index[0, d + 16]
                    block = jnp.where(left, acc2[one], acc2[two]).astype(BF16)
                    stat = jnp.where(left1, lse2[one], lse2[two])
                    sa[hi, dx, dy * 2 + zp] = block[:64]
                    sb[hi, dy, dx * 2 + zp] = block[64:]
                    la[hi, dx, pl.ds(dy * 2 + zp, 1), :] = stat
                    lb[hi, dy, pl.ds(dx * 2 + zp, 1), :] = stat
                return carry

            lax.fori_loop(0, 4, place_step, 0)

    def send_first(hi):
        sent = []
        for k in range(3):
            to_x, to_y = (x + k + 1) % 4, (y + k + 1) % 4
            for m, (src, dst, peer) in enumerate((
                (sa.at[hi, to_x], ra.at[hi, k], x_peers[k]),
                (sb.at[hi, to_y], rb.at[hi, k], y_peers[k]),
                (la.at[hi, to_x], rla.at[hi, k], x_peers[k]),
                (lb.at[hi, to_y], rlb.at[hi, k], y_peers[k]),
            )):
                sent.append(remote(src, dst, r1_ssem.at[hi, m, k], r1_rsem.at[hi, m, k], peer))
        for copy in sent:
            copy.start()
        return sent

    def merge_first(hi):
        for mine_s, mine_l, got_s, got_l, where, next_s, next_l in (
            (sa, la, ra, rla, x, sa2, la2), (sb, lb, rb, rlb, y, sb2, lb2)
        ):
            weights, joined = shares([mine_l[hi, where]] + [got_l[hi, k] for k in range(3)])
            for t in range(8):
                block = mine_s[hi, where, t].astype(F32) * weights[0][t : t + 1]
                for k in range(3):
                    block = block + got_s[hi, k, t].astype(F32) * weights[k + 1][t : t + 1]
                next_s[hi, t // 2, t % 2] = block.astype(BF16)
            for group in range(4):
                next_l[hi, group] = jnp.concatenate([joined[group * 2 : group * 2 + 2], zeros6], axis=0)

    def send_second(hi):
        sent = []
        for k in range(3):
            to_x, to_y = (x + k + 1) % 4, (y + k + 1) % 4
            for m, (src, dst, peer) in enumerate((
                (sa2.at[hi, to_y], ra2.at[hi, k], y_peers[k]),
                (sb2.at[hi, to_x], rb2.at[hi, k], x_peers[k]),
                (la2.at[hi, to_y], rla2.at[hi, k], y_peers[k]),
                (lb2.at[hi, to_x], rlb2.at[hi, k], x_peers[k]),
            )):
                sent.append(remote(src, dst, r2_ssem.at[hi, m, k], r2_rsem.at[hi, m, k], peer))
        for copy in sent:
            copy.start()
        return sent

    def merge_second(hi):
        sides = []
        for mine_s, mine_l, got_s, got_l, where in ((sa2, la2, ra2, rla2, y), (sb2, lb2, rb2, rlb2, x)):
            weights, joined = shares([mine_l[hi, where]] + [got_l[hi, k] for k in range(3)])
            blocks = []
            for zp in range(2):
                block = mine_s[hi, where, zp].astype(F32) * weights[0][zp : zp + 1]
                for k in range(3):
                    block = block + got_s[hi, k, zp].astype(F32) * weights[k + 1][zp : zp + 1]
                blocks.append(block)
            sides.append((blocks, joined))
        for zp in range(2):
            a, b = sides[0][0][zp], sides[1][0][zp]
            s3[hi * 4 + zp * 2] = jnp.where(left64, a, pltpu.roll(b, 64, 1)).astype(BF16)
            s3[hi * 4 + zp * 2 + 1] = jnp.where(left64, pltpu.roll(a, 64, 1), b).astype(BF16)
            a, b = sides[0][1], sides[1][1]
            l3[hi * 4 + zp * 2] = jnp.where(lane8 < 64, a, pltpu.roll(b, 64, 1))[zp : zp + 1]
            l3[hi * 4 + zp * 2 + 1] = jnp.where(lane8 < 64, pltpu.roll(a, 64, 1), b)[zp : zp + 1]

    for copy in g3[0]:
        copy.wait_recv()
    prompt_part(0)
    r1_low = send_first(0)
    for copy in g3[1]:
        copy.wait_recv()
    prompt_part(1)
    r1_high = send_first(1)
    for copy in gz + g2[0] + g2[1] + g3[0] + g3[1] + mig + core_copies:
        copy.wait_send()
    for copy in ret:
        copy.wait_recv()
    back = [ret_rcv[bit, s].astype(F32) for s in range(4)]
    for j in range(4):
        for s in range(4):
            out[j, s] = jnp.where(my_slot == j, back[s], ret_loc[j, s].astype(F32)).astype(BF16)
    for copy in r1_low:
        copy.wait_recv()
    merge_first(0)
    r2_low = send_second(0)
    for copy in r1_high:
        copy.wait_recv()
    merge_first(1)
    r2_high = send_second(1)
    for copy in r2_low:
        copy.wait_recv()
    merge_second(0)
    for copy in r2_high:
        copy.wait_recv()
    merge_second(1)

    rz = []
    for k in range(7):
        to = (z + k + 1) % 8
        rz.append(remote(s3.at[to], r3.at[k], rz_ssem.at[0, k], rz_rsem.at[0, k], z_peers[k]))
        rz.append(remote(l3.at[to], rl3.at[k], rz_ssem.at[1, k], rz_rsem.at[1, k], z_peers[k]))
    for copy in rz:
        copy.start()
    for copy in r1_low + r1_high + r2_low + r2_high + ret:
        copy.wait_send()
    for copy in rz:
        copy.wait_recv()
    weights, _ = shares([new_lse, l3[z]] + [rl3[k] for k in range(7)])
    block = new_acc * weights[0] + s3[z].astype(F32) * weights[1]
    for k in range(7):
        block = block + r3[k].astype(F32) * weights[k + 2]
    flat = jnp.concatenate([block, block], axis=0).T
    here = jnp.where(left64, flat[:64], flat[64:])
    for s in range(4):
        out[4, s] = jnp.concatenate([here[s * 8 : s * 8 + 8], here[32 + s * 8 : 40 + s * 8]], axis=0).astype(BF16)
    for copy in rz:
        copy.wait_send()


def per_device(
    pool_kv, block_table, context_len, partner, mig_slot, prompt_kv, prompt_dest, queries, step_kv
):
    vmem = pl.BlockSpec(memory_space=pltpu.VMEM)
    hbm = pl.BlockSpec(memory_space=pltpu.HBM)
    sem = lambda *shape: pltpu.SemaphoreType.DMA(shape)
    V = pltpu.VMEM
    return pl.pallas_call(
        body,
        out_shape=jax.ShapeDtypeStruct((5, 4, 16, HD), BF16),
        in_specs=[hbm] * 11,
        out_specs=vmem,
        scratch_shapes=[
            pltpu.SMEM((3072,), jnp.int32),
            pltpu.SMEM((4, 64), jnp.int32),
            pltpu.SMEM((64,), jnp.int32),
            pltpu.SMEM((64,), jnp.int32),
            pltpu.SMEM((4, 24), jnp.int32),
            V((24, HD), jnp.int32),
            V((1, HD), F32),
            V((5, 4, 16, HD), BF16),
            V((5, 16, HD), BF16),
            V((48, 2, 2, 64, HD), BF16),
            V((2, 2, 12, 2, 2, 64, HD), BF16),
            V((12, 8, HD), F32),
            V((8, HD), jnp.int32),
            pltpu.SMEM((8, HD), jnp.int32),
            V((4, 80, HD), BF16),
            V((80, HD), BF16),
            V((3, 80, HD), BF16),
            V((4, 4, 16, HD), BF16),
            V((4, 16, HD), BF16),
            V((3, 4, 16, HD), BF16),
            V((8, 64, HD), BF16),
            V((4, 4, 4, 32, HD), BF16),
            V((4, 4, 4, 32, HD), BF16),
            V((4, 4, 4, 32, HD), BF16),
            V((4, 4, 4, 32, HD), BF16),
            V((25, HD, HD), F32),
            V((25, 1, HD), F32),
            V((25, HD, HD), F32),
            V((25, 1, HD), F32),
            V((2, 4, 8, 64, HD), BF16),
            V((2, 4, 8, 64, HD), BF16),
            V((2, 4, 8, HD), F32),
            V((2, 4, 8, HD), F32),
            V((2, 3, 8, 64, HD), BF16),
            V((2, 3, 8, 64, HD), BF16),
            V((2, 3, 8, HD), F32),
            V((2, 3, 8, HD), F32),
            V((2, 4, 2, 64, HD), BF16),
            V((2, 4, 2, 64, HD), BF16),
            V((2, 4, 8, HD), F32),
            V((2, 4, 8, HD), F32),
            V((2, 3, 2, 64, HD), BF16),
            V((2, 3, 2, 64, HD), BF16),
            V((2, 3, 8, HD), F32),
            V((2, 3, 8, HD), F32),
            V((8, 64, HD), BF16),
            V((8, 1, HD), F32),
            V((7, 64, HD), BF16),
            V((7, 1, HD), F32),
            sem(9), sem(4), sem(2), sem(2), sem(3), sem(3), sem(3), sem(3),
            sem(7), sem(7), sem(2, 2, 3), sem(2, 2, 3), sem(2, 2, 3), sem(2, 2, 3),
            sem(2, 4, 3), sem(2, 4, 3), sem(2, 4, 3), sem(2, 4, 3), sem(2, 7), sem(2, 7),
        ],
        compiler_params=pltpu.CompilerParams(
            collective_id=0, has_side_effects=True, vmem_limit_bytes=60 * 1024 * 1024
        ),
    )(
        prompt_dest.reshape(-1), context_len.T, partner, mig_slot, block_table,
        prompt_dest.reshape(24, HD), jnp.asarray(rope_row()), queries, step_kv.reshape(5, 16, HD),
        pool_kv, prompt_kv,
    )


def solution(mesh):
    placed = (
        P("inst", None, "tp", None, None),
        P("inst", None),
        P(),
        P(),
        P(),
        P(("inst", "tp"), None, None, None, None),
        P(),
        P("inst", None, "tp", None),
        P("inst", None, None, "tp", None),
    )
    return jax.shard_map(
        per_device,
        mesh=mesh,
        in_specs=placed,
        out_specs=P("inst", None, "tp", None),
        check_vma=False,
    )
```

```python
import math

import jax
import jax.numpy as jnp
import numpy as np
from jax import lax
from jax.experimental import pallas as pl
from jax.experimental.pallas import tpu as pltpu
from jax.sharding import PartitionSpec as P

MESH = pl.DeviceIdType.MESH
NEG = -1e30
F32 = jnp.float32
BF16 = jnp.bfloat16
HD = 128
SCALE = 1.0 / math.sqrt(HD)
UNROLL = 3


def rope_row():
    ratio = np.arange(HD // 2) * (2.0 / HD)
    base = np.exp(-ratio * math.log(500000.0))
    wavelength = 2.0 * math.pi / base
    smooth = (8192.0 / wavelength - 1.0) / 3.0
    blended = (1.0 - smooth) * base / 8.0 + smooth * base
    freqs = np.where(wavelength < 2048.0, base, np.where(wavelength > 8192.0, base / 8.0, blended))
    return np.concatenate([freqs, freqs])[None].astype(np.float32)


def cos_sin(angle):
    turns = jnp.floor(angle * (2.0 / math.pi) + 0.5)
    r = angle - turns * 1.5703125
    r = r - turns * 4.837512969970703125e-4
    r = r - turns * 7.54978995489188216e-8
    sq = r * r
    sine = ((-1.9515295891e-4 * sq + 8.3321608736e-3) * sq - 1.6666654611e-1) * sq * r + r
    cosine = (2.443315711809948e-5 * sq - 1.388731625493765e-3) * sq + 4.166664568298827e-2
    cosine = cosine * sq * sq - 0.5 * sq + 1.0
    quarter = turns - 4.0 * jnp.floor(turns * 0.25)
    odd = (quarter == 1.0) | (quarter == 3.0)
    first, second = jnp.where(odd, sine, cosine), jnp.where(odd, cosine, sine)
    first = jnp.where((quarter == 1.0) | (quarter == 2.0), -first, first)
    second = jnp.where(quarter >= 2.0, -second, second)
    return first, second


def dot_nn(a, b):
    return lax.dot_general(a, b, (((1,), (0,)), ((), ())), preferred_element_type=F32)


def dot_tn(a, b):
    return lax.dot_general(a, b, (((0,), (0,)), ((), ())), preferred_element_type=F32)


def shares(parts):
    top = parts[0]
    for part in parts[1:]:
        top = jnp.maximum(top, part)
    weights = [jnp.exp(part - top) for part in parts]
    total = weights[0]
    for part in weights[1:]:
        total = total + part
    return [part / total for part in weights], top + jnp.log(total)


def iota(shape, axis):
    return lax.broadcasted_iota(jnp.int32, shape, axis)


def body(
    dests_in, lengths_in, partner_in, mig_slot_in, table_in, grid_in, freqs_in, queries_in, kv_in,
    pool_hbm, prompt_hbm, out,
    dests, lengths, partner, mig_slot, table, dest_grid, freqs, queries, step_kv,
    pool, pages, ab, index_v, index, mig_mine, mig_send, mig_rcv, ret_loc, ret_send, ret_rcv,
    zq, qa_low, qa_high, qb_low, qb_high, acc, lse, acc2, lse2,
    sa, sb, la, lb, ra, rb, rla, rlb, ma, mb, mla, mlb,
    sa2, sb2, la2, lb2, ra2, rb2, rla2, rlb2,
    s3, l3, r3, rl3,
    in_sem, local_sem, core_ssem, core_rsem, mig_ssem, mig_rsem, ret_ssem, ret_rsem,
    gz_ssem, gz_rsem, g2_ssem, g2_rsem, g3_ssem, g3_rsem,
    r1_ssem, r1_rsem, r2_ssem, r2_rsem, rz_ssem, rz_rsem,
):
    inst = lax.axis_index("inst")
    tp = lax.axis_index("tp")
    z_lo, y, x = inst // 16, (inst // 4) % 4, inst % 4
    z_hi, core = tp // 2, tp % 2
    z = z_hi * 4 + z_lo

    def device(zz, yy, xx, cc):
        return ((zz % 4) * 16 + yy * 4 + xx, (zz // 4) * 2 + cc)

    x_peers = [device(z, y, (x + k) % 4, core) for k in (1, 2, 3)]
    y_peers = [device(z, (y + k) % 4, x, core) for k in (1, 2, 3)]
    z_peers = [device((z + k) % 8, y, x, core) for k in range(1, 8)]
    core_peer = device(z, y, x, 1 - core)
    mig_peers = [
        device(z, y, x + 1 - 2 * (x % 2), core),
        device(z, y, (x + 2) % 4, core),
        device(z, y + 1 - 2 * (y % 2), x, core),
    ]

    barrier = pltpu.get_barrier_semaphore()
    everyone = [core_peer] + x_peers + y_peers + z_peers
    for peer in everyone:
        pl.semaphore_signal(barrier, inc=1, device_id=peer, device_id_type=MESH)

    def remote(src, dst, ssem, rsem, peer):
        return pltpu.make_async_remote_copy(
            src_ref=src, dst_ref=dst, send_sem=ssem, recv_sem=rsem,
            device_id=peer, device_id_type=MESH,
        )

    inputs = [
        pltpu.make_async_copy(src, dst, in_sem.at[n])
        for n, (src, dst) in enumerate((
            (grid_in, dest_grid), (freqs_in, freqs), (queries_in, queries), (mig_slot_in, mig_slot),
            (partner_in, partner), (lengths_in, lengths), (dests_in, dests), (table_in, table), (kv_in, step_kv),
        ))
    ]
    for copy in inputs:
        copy.start()
    pool_copy = pltpu.make_async_copy(pool_hbm, pool, local_sem.at[0])
    pool_copy.start()
    own_copies = [
        pltpu.make_async_copy(
            prompt_hbm.at[:, :, pl.ds(hi * 4 + core * 2, 2)], pages.at[core, hi], local_sem.at[1 + hi]
        )
        for hi in range(2)
    ]
    for copy in own_copies:
        copy.start()

    first_row = inst * 48 + z_hi * 24

    for copy in inputs[:3]:
        copy.wait()
    freq = freqs[...]
    lane8 = iota((8, HD), 1)
    line8 = iota((8, HD), 0)
    line16 = iota((16, HD), 0)
    sign = jnp.where(lane8[:1] < 64, -1.0, 1.0)
    is_key = (line16 // 2) % 2 == 0

    def tables(length):
        at = length + (line8 % 4).astype(F32)
        cosine, sine = cos_sin(at * freq)
        return cosine, sine * sign

    def key_tables(length):
        at = jnp.where(is_key, length + (line16 // 4).astype(F32), 0.0)
        cosine, sine = cos_sin(at * freq)
        return cosine, sine * sign

    def turn(value, cosine, sine):
        return value * cosine + pltpu.roll(value, 64, 1) * sine

    def turned_query(slot, cosine, sine):
        tiles = [[None] * 4, [None] * 4]
        for s in range(4):
            both = queries[slot, s].astype(F32)
            for h in range(2):
                tiles[h][s] = turn(both[h * 8 : h * 8 + 8], cosine[s : s + 1], sine[s : s + 1])
        return [jnp.concatenate(part, axis=0) for part in tiles]

    named_here = jnp.where(dest_grid[...] == inst, 1.0, 0.0)
    new_len = jnp.sum(jnp.sum(named_here, axis=0, keepdims=True), axis=1, keepdims=True) * 64.0
    mine = turned_query(4, *tables(new_len))
    twice = jnp.concatenate(mine + mine, axis=0).T
    zq[z] = jnp.where(iota((64, HD), 1) < 64, twice[:64], twice[64:]).astype(BF16)
    twice = twice.astype(BF16)
    qa, qb = (qa_low, qa_high), (qb_low, qb_high)

    pl.semaphore_wait(barrier, len(everyone))

    gz = []
    for k in range(7):
        gz.append(remote(zq.at[z], zq.at[z], gz_ssem.at[k], gz_rsem.at[k], z_peers[k]))
    for copy in gz:
        copy.start()
    for copy in inputs[3:]:
        copy.wait()

    my_slot = mig_slot[inst]
    mate = partner[inst]
    mate_len = lengths[mig_slot[mate], mate]
    own_len = [lengths[j, inst] for j in range(4)]
    bit = jnp.where(mate // 4 != inst // 4, 2, jnp.where(mate // 2 != inst // 2, 1, 0))

    for j in range(4):
        length = jnp.where(my_slot == j, mate_len, own_len[j]).astype(F32)
        part = turned_query(j, *tables(length))
        mig_mine[j, pl.ds(0, 32)] = part[0].astype(BF16)
        mig_mine[j, pl.ds(32, 32)] = part[1].astype(BF16)
        mig_mine[j, pl.ds(64, 16)] = turn(step_kv[j].astype(F32), *key_tables(length)).astype(BF16)
    mig_send[...] = mig_mine[my_slot]
    mig = [remote(mig_send, mig_rcv.at[k], mig_ssem.at[k], mig_rsem.at[k], mig_peers[k]) for k in range(3)]
    for copy in mig:
        copy.start()
    core_copies = [
        remote(
            prompt_hbm.at[:, :, pl.ds(hi * 4 + (1 - core) * 2, 2)],
            pages.at[core, hi], core_ssem.at[hi], core_rsem.at[hi], core_peer,
        )
        for hi in range(2)
    ]
    for copy in core_copies:
        copy.start()

    first = jnp.full((8, HD), 24, jnp.int32)
    second = jnp.full((8, HD), 24, jnp.int32)
    for n in range(24):
        hit = lane8 == dests[first_row + n]
        second = jnp.where(hit & (first < 24), n, second)
        first = jnp.where(hit & (first == 24), n, first)
    index_v[...] = jnp.where(line8 == 0, first, second)
    index_copy = pltpu.make_async_copy(index_v, index, local_sem.at[3])
    index_copy.start()

    own_kv = turn(step_kv[4].astype(F32), *key_tables(new_len)).astype(BF16)
    lane16 = iota((16, HD), 1)
    ok = is_key & (line16 % 2 == (lane16 % 64) // 32) & (line16 // 4 <= (lane16 % 32) // 8)
    score = jnp.where(ok, dot_nn(own_kv, twice) * SCALE, NEG)
    top = jnp.max(score, axis=0, keepdims=True)
    weight = jnp.where(ok, jnp.exp(score - top), 0.0).astype(BF16).astype(F32)
    total = jnp.sum(weight, axis=0, keepdims=True)
    new_acc = dot_tn(own_kv, pltpu.roll(weight, 2, 0).astype(BF16)) / total
    new_acc = jnp.where(iota((64, HD), 1) < 64, new_acc[:64], new_acc[64:])
    new_lse = top + jnp.log(total)

    shape = (12, 8, HD)
    row = iota(shape, 1)
    page_id = iota(shape, 0) * 4 + row % 4
    is_last = row // 4
    lane1 = lane8[:1]

    def by_slot(values):
        return jnp.where(
            lane1 < 64, jnp.where(lane1 < 32, values[0], values[1]), jnp.where(lane1 < 96, values[2], values[3])
        )

    context = by_slot(own_len)
    full, rem = context // 64, context % 64
    ab[...] = jnp.zeros(shape, F32)

    def count_step(k, carry):
        named = by_slot([table[j, k] for j in range(4)])[None]
        kind = jnp.where(k < full, 0, jnp.where(k == full, 1, 2))[None]
        hit = (page_id == named) & (is_last == kind)
        ab[...] += jnp.where(hit, 1.0, 0.0)
        return carry

    lax.fori_loop(0, 24, count_step, 0)

    for copy in gz:
        copy.wait_recv()
    g2 = [[], []]
    for hi in range(2):
        part = zq.at[pl.ds(hi * 4, 4), pl.ds(0, 32)]
        other = zq.at[pl.ds(hi * 4, 4), pl.ds(32, 32)]
        for k in range(3):
            g2[hi].append(remote(part, qa[hi].at[x, y], g2_ssem.at[hi, 0, k], g2_rsem.at[hi, 0, k], y_peers[k]))
            g2[hi].append(remote(other, qb[hi].at[y, x], g2_ssem.at[hi, 1, k], g2_rsem.at[hi, 1, k], x_peers[k]))
        for copy in g2[hi]:
            copy.start()
    for hi in range(2):
        qa[hi][x, y] = zq[pl.ds(hi * 4, 4), pl.ds(0, 32)]
        qb[hi][y, x] = zq[pl.ds(hi * 4, 4), pl.ds(32, 32)]
    for copy in mig:
        copy.wait_recv()

    came = mig_rcv[bit].astype(F32)
    blocks = [jnp.where(my_slot == j, came, mig_mine[j].astype(F32)) for j in range(4)]
    fresh_kv = jnp.concatenate([block[64:80] for block in blocks], axis=0).astype(BF16)
    q_res = [
        jnp.concatenate([block[h * 32 : h * 32 + 32] for block in blocks], axis=0).T.astype(BF16) for h in range(2)
    ]
    pool_copy.wait()
    below = (iota((64, HD), 0) < rem).astype(F32)

    def res_step(i, carry):
        named = ab[i]
        count = (named[0:4][:, None, :] + named[4:8][:, None, :] * below[None]).reshape(256, HD)
        real = count > 0.0
        after = []
        for h in range(2):
            best, total, summed = carry[3 * h : 3 * h + 3]
            keys = pool[pl.ds(i * 4, 4), 0, h].reshape(256, HD)
            values = pool[pl.ds(i * 4, 4), 1, h].reshape(256, HD)
            score = jnp.where(real, dot_nn(keys, q_res[h]) * SCALE, NEG)
            top = jnp.maximum(best, jnp.max(score, axis=0, keepdims=True))
            weight = (count * jnp.exp(score - top)).astype(BF16)
            shrink = jnp.exp(best - top)
            total = total * shrink + jnp.sum(weight.astype(F32), axis=0, keepdims=True)
            summed = summed * shrink + dot_tn(values, weight)
            after += [top, total, summed]
        return tuple(after)

    start = (jnp.full((1, HD), NEG, F32), jnp.zeros((1, HD), F32), jnp.zeros((HD, HD), F32)) * 2
    state = lax.fori_loop(0, 4, res_step, start)
    right = ((x + 1) % 4, (y + 1) % 4)
    left_by = ((x + 3) % 4, (y + 3) % 4)
    right_peer, left_peer = (x_peers[0], y_peers[0]), (x_peers[2], y_peers[2])
    place = (x, y)

    def ring(hi, side, kind, row, peer):
        part = (qa, qb)[side][hi].at[row]
        return remote(part, part, g3_ssem.at[hi, side, kind], g3_rsem.at[hi, side, kind], peer)

    g3 = [
        [[ring(hi, side, 0, place[side], right_peer[side]) for side in range(2)],
         [ring(hi, side, 1, place[side], left_peer[side]) for side in range(2)],
         [ring(hi, side, 2, (left_by, right)[hi][side], (right_peer, left_peer)[hi][side]) for side in range(2)]]
        for hi in range(2)
    ]
    for copy in g2[0]:
        copy.wait_recv()
    for copy in g3[0][0] + g3[0][1]:
        copy.start()
    for copy in g2[1]:
        copy.wait_recv()
    for copy in g3[1][1]:
        copy.start()
    state = lax.fori_loop(4, 8, res_step, state)
    for copy in g3[0][0]:
        copy.wait_recv()
    for copy in g3[0][2] + g3[1][0]:
        copy.start()
    state = lax.fori_loop(8, 12, res_step, state)
    lane = iota((64, HD), 1)
    line = iota((64, HD), 0)
    ok_slot = (line // 16 == lane // 32) & ((line // 2) % 2 == 0) & ((line % 16) // 4 <= (lane % 32) // 8)
    rows = []
    for h in range(2):
        best, total, summed = state[3 * h : 3 * h + 3]
        ok = ok_slot & (line % 2 == h)
        score = jnp.where(ok, dot_nn(fresh_kv, q_res[h]) * SCALE, NEG)
        top = jnp.maximum(best, jnp.max(score, axis=0, keepdims=True))
        weight = jnp.where(ok, jnp.exp(score - top), 0.0).astype(BF16).astype(F32)
        shrink = jnp.exp(best - top)
        total = total * shrink + jnp.sum(weight, axis=0, keepdims=True)
        summed = summed * shrink + dot_tn(fresh_kv, pltpu.roll(weight, 2, 0).astype(BF16))
        rows.append((summed / total).T)
    for j in range(4):
        for s in range(4):
            at = j * 32 + s * 8
            ret_loc[j, s] = jnp.concatenate([rows[0][at : at + 8], rows[1][at : at + 8]], axis=0).astype(BF16)
    ret_send[...] = ret_loc[my_slot]
    ret = [remote(ret_send, ret_rcv.at[k], ret_ssem.at[k], ret_rsem.at[k], mig_peers[k]) for k in range(3)]
    for copy in ret:
        copy.start()

    for copy in g3[1][1]:
        copy.wait_recv()
    for copy in g3[1][2]:
        copy.start()

    for copy in own_copies:
        copy.wait()
    for copy in core_copies:
        copy.wait_recv()
    index_copy.wait()
    acc[24] = jnp.zeros((HD, HD), F32)
    acc2[24] = jnp.zeros((HD, HD), F32)
    lse[24] = jnp.full((1, HD), NEG, F32)
    lse2[24] = jnp.full((1, HD), NEG, F32)
    same_head = iota((HD, HD), 0) // 64 == (iota((HD, HD), 1) % 64) // 32
    left = iota((HD, HD), 1) < 64
    left1 = lane1 < 64
    left64 = lane < 64
    zeros6 = jnp.zeros((6, HD), F32)

    def prompt_part(hi):
        def page(n, src, i):
            d = dests[first_row + n]
            zl, dy, dx = d // 16, (d // 4) % 4, d % 4
            part = jnp.concatenate([qa[hi][dx, dy, zl], qb[hi][dy, dx, zl]], axis=0)
            swap = jnp.concatenate([part[:, 64:], part[:, :64]], axis=1)
            asked = jnp.concatenate([jnp.where(left64, part, swap), jnp.where(left64, swap, part)], axis=0)
            score = jnp.where(same_head, dot_nn(pages[src, hi, i, 0].reshape(HD, HD), asked) * SCALE, NEG)
            top = jnp.max(score, axis=0, keepdims=True)
            weight = jnp.exp(score - top).astype(BF16)
            total = jnp.sum(weight.astype(F32), axis=0, keepdims=True)
            acc[n] = dot_tn(pages[src, hi, i, 1].reshape(HD, HD), weight) / total
            lse[n] = top + jnp.log(total)

        def page_step(i, carry):
            for src in range(2):
                for more in range(UNROLL):
                    page(src * 12 + i * UNROLL + more, src, i * UNROLL + more)
            return carry

        lax.fori_loop(0, 12 // UNROLL, page_step, 0)

        def join_step(i, carry):
            for more in range(4):
                n = i * 4 + more
                d = dests[first_row + n]
                first = index[0, d]
                other = jnp.where(first == n, index[1, d], first)
                weights, joined = shares([lse[n], lse[other]])
                acc2[n] = acc[n] * weights[0] + acc[other] * weights[1]
                lse2[n] = joined
            return carry

        lax.fori_loop(0, 6, join_step, 0)

        for zp in range(2):
            def place_step(dy, carry):
                for dx in range(4):
                    d = zp * 32 + dy * 4 + dx
                    one, two = index[0, d], index[0, d + 16]
                    block = jnp.where(left, acc2[one], acc2[two]).astype(BF16)
                    stat = jnp.where(left1, lse2[one], lse2[two])
                    sa[hi, dx, dy * 2 + zp] = block[:64]
                    sb[hi, dy, dx * 2 + zp] = block[64:]
                    la[hi, dx, pl.ds(dy * 2 + zp, 1), :] = stat
                    lb[hi, dy, pl.ds(dx * 2 + zp, 1), :] = stat
                return carry

            lax.fori_loop(0, 4, place_step, 0)

    sides = ((sa, la, ra, rla, ma, mla, x, sa2, la2), (sb, lb, rb, rlb, mb, mlb, y, sb2, lb2))

    def first_copies(hi, side, kind, data, stat, peer):
        _, _, got_s, got_l = sides[side][:4]
        return [
            remote(data, got_s.at[hi, kind], r1_ssem.at[hi, side, kind], r1_rsem.at[hi, side, kind], peer),
            remote(stat, got_l.at[hi, kind], r1_ssem.at[hi, 2 + side, kind], r1_rsem.at[hi, 2 + side, kind], peer),
        ]

    def send_first(hi):
        sent = [[], []]
        for side in range(2):
            mine_s, mine_l = sides[side][:2]
            ahead, behind = (right_peer, left_peer) if hi == 0 else (left_peer, right_peer)
            back = ((left_by, right)[hi])[side]
            far = (place[side] + 2) % 4
            sent[0] += first_copies(hi, side, 0, mine_s.at[hi, far], mine_l.at[hi, far], ahead[side])
            sent[1] += first_copies(hi, side, 1, mine_s.at[hi, back], mine_l.at[hi, back], behind[side])
        for copy in sent[0] + sent[1]:
            copy.start()
        return sent

    def pass_on(hi):
        sent = []
        for side in range(2):
            mine_s, mine_l, got_s, got_l, mid_s, mid_l = sides[side][:6]
            front = ((right, left_by)[hi])[side]
            weights, joined = shares([mine_l[hi, front], got_l[hi, 0]])
            for t in range(8):
                block = mine_s[hi, front, t].astype(F32) * weights[0][t : t + 1]
                block = block + got_s[hi, 0, t].astype(F32) * weights[1][t : t + 1]
                mid_s[hi, t] = block.astype(BF16)
            mid_l[hi] = joined
            ahead = (right_peer, left_peer)[hi][side]
            sent += first_copies(hi, side, 2, mid_s.at[hi], mid_l.at[hi], ahead)
            for copy in sent[-2:]:
                copy.start()
        return sent

    def merge_first(hi):
        for mine_s, mine_l, got_s, got_l, _, _, where, next_s, next_l in sides:
            weights, joined = shares([mine_l[hi, where], got_l[hi, 1], got_l[hi, 2]])
            for t in range(8):
                block = mine_s[hi, where, t].astype(F32) * weights[0][t : t + 1]
                for k in range(1, 3):
                    block = block + got_s[hi, k, t].astype(F32) * weights[k][t : t + 1]
                next_s[hi, t // 2, t % 2] = block.astype(BF16)
            for group in range(4):
                next_l[hi, group] = jnp.concatenate([joined[group * 2 : group * 2 + 2], zeros6], axis=0)

    def send_second(hi):
        sent = []
        for k in range(3):
            to_x, to_y = (x + k + 1) % 4, (y + k + 1) % 4
            for m, (src, dst, peer) in enumerate((
                (sa2.at[hi, to_y], ra2.at[hi, k], y_peers[k]),
                (sb2.at[hi, to_x], rb2.at[hi, k], x_peers[k]),
                (la2.at[hi, to_y], rla2.at[hi, k], y_peers[k]),
                (lb2.at[hi, to_x], rlb2.at[hi, k], x_peers[k]),
            )):
                sent.append(remote(src, dst, r2_ssem.at[hi, m, k], r2_rsem.at[hi, m, k], peer))
        for copy in sent:
            copy.start()
        return sent

    def merge_second(hi):
        both = []
        for mine_s, mine_l, got_s, got_l, where in ((sa2, la2, ra2, rla2, y), (sb2, lb2, rb2, rlb2, x)):
            weights, joined = shares([mine_l[hi, where]] + [got_l[hi, k] for k in range(3)])
            blocks = []
            for zp in range(2):
                block = mine_s[hi, where, zp].astype(F32) * weights[0][zp : zp + 1]
                for k in range(3):
                    block = block + got_s[hi, k, zp].astype(F32) * weights[k + 1][zp : zp + 1]
                blocks.append(block)
            both.append((blocks, joined))
        for zp in range(2):
            a, b = both[0][0][zp], both[1][0][zp]
            s3[hi * 4 + zp * 2] = jnp.where(left64, a, pltpu.roll(b, 64, 1)).astype(BF16)
            s3[hi * 4 + zp * 2 + 1] = jnp.where(left64, pltpu.roll(a, 64, 1), b).astype(BF16)
            a, b = both[0][1], both[1][1]
            l3[hi * 4 + zp * 2] = jnp.where(lane8 < 64, a, pltpu.roll(b, 64, 1))[zp : zp + 1]
            l3[hi * 4 + zp * 2 + 1] = jnp.where(lane8 < 64, pltpu.roll(a, 64, 1), b)[zp : zp + 1]

    for copy in g3[0][1] + g3[0][2]:
        copy.wait_recv()
    prompt_part(0)
    r1_low = send_first(0)
    for copy in g3[1][0] + g3[1][2]:
        copy.wait_recv()
    prompt_part(1)
    r1_high = send_first(1)
    for copy in r1_low[0]:
        copy.wait_recv()
    r1_low.append(pass_on(0))
    for copy in r1_high[0]:
        copy.wait_recv()
    r1_high.append(pass_on(1))
    for copy in gz + g2[0] + g2[1] + g3[0][0] + g3[0][1] + g3[0][2] + g3[1][0] + g3[1][1] + g3[1][2] + mig + core_copies:
        copy.wait_send()
    for copy in ret:
        copy.wait_recv()
    back = [ret_rcv[bit, s].astype(F32) for s in range(4)]
    for j in range(4):
        for s in range(4):
            out[j, s] = jnp.where(my_slot == j, back[s], ret_loc[j, s].astype(F32)).astype(BF16)
    for copy in r1_low[1] + r1_low[2]:
        copy.wait_recv()
    merge_first(0)
    r2_low = send_second(0)
    for copy in r1_high[1] + r1_high[2]:
        copy.wait_recv()
    merge_first(1)
    r2_high = send_second(1)
    for copy in r2_low:
        copy.wait_recv()
    merge_second(0)
    for copy in r2_high:
        copy.wait_recv()
    merge_second(1)

    rz = []
    for k in range(7):
        to = (z + k + 1) % 8
        rz.append(remote(s3.at[to], r3.at[k], rz_ssem.at[0, k], rz_rsem.at[0, k], z_peers[k]))
        rz.append(remote(l3.at[to], rl3.at[k], rz_ssem.at[1, k], rz_rsem.at[1, k], z_peers[k]))
    for copy in rz:
        copy.start()
    for copy in sum(r1_low + r1_high, []) + r2_low + r2_high + ret:
        copy.wait_send()
    for copy in rz:
        copy.wait_recv()
    weights, _ = shares([new_lse, l3[z]] + [rl3[k] for k in range(7)])
    block = new_acc * weights[0] + s3[z].astype(F32) * weights[1]
    for k in range(7):
        block = block + r3[k].astype(F32) * weights[k + 2]
    flat = jnp.concatenate([block, block], axis=0).T
    here = jnp.where(left64, flat[:64], flat[64:])
    for s in range(4):
        out[4, s] = jnp.concatenate([here[s * 8 : s * 8 + 8], here[32 + s * 8 : 40 + s * 8]], axis=0).astype(BF16)
    for copy in rz:
        copy.wait_send()


def per_device(
    pool_kv, block_table, context_len, partner, mig_slot, prompt_kv, prompt_dest, queries, step_kv
):
    vmem = pl.BlockSpec(memory_space=pltpu.VMEM)
    hbm = pl.BlockSpec(memory_space=pltpu.HBM)
    sem = lambda *shape: pltpu.SemaphoreType.DMA(shape)
    V = pltpu.VMEM
    return pl.pallas_call(
        body,
        out_shape=jax.ShapeDtypeStruct((5, 4, 16, HD), BF16),
        in_specs=[hbm] * 11,
        out_specs=vmem,
        scratch_shapes=[
            pltpu.SMEM((3072,), jnp.int32),
            pltpu.SMEM((4, 64), jnp.int32),
            pltpu.SMEM((64,), jnp.int32),
            pltpu.SMEM((64,), jnp.int32),
            pltpu.SMEM((4, 24), jnp.int32),
            V((24, HD), jnp.int32),
            V((1, HD), F32),
            V((5, 4, 16, HD), BF16),
            V((5, 16, HD), BF16),
            V((48, 2, 2, 64, HD), BF16),
            V((2, 2, 12, 2, 2, 64, HD), BF16),
            V((12, 8, HD), F32),
            V((8, HD), jnp.int32),
            pltpu.SMEM((8, HD), jnp.int32),
            V((4, 80, HD), BF16),
            V((80, HD), BF16),
            V((3, 80, HD), BF16),
            V((4, 4, 16, HD), BF16),
            V((4, 16, HD), BF16),
            V((3, 4, 16, HD), BF16),
            V((8, 64, HD), BF16),
            V((4, 4, 4, 32, HD), BF16),
            V((4, 4, 4, 32, HD), BF16),
            V((4, 4, 4, 32, HD), BF16),
            V((4, 4, 4, 32, HD), BF16),
            V((25, HD, HD), F32),
            V((25, 1, HD), F32),
            V((25, HD, HD), F32),
            V((25, 1, HD), F32),
            V((2, 4, 8, 64, HD), BF16),
            V((2, 4, 8, 64, HD), BF16),
            V((2, 4, 8, HD), F32),
            V((2, 4, 8, HD), F32),
            V((2, 3, 8, 64, HD), BF16),
            V((2, 3, 8, 64, HD), BF16),
            V((2, 3, 8, HD), F32),
            V((2, 3, 8, HD), F32),
            V((2, 8, 64, HD), BF16),
            V((2, 8, 64, HD), BF16),
            V((2, 8, HD), F32),
            V((2, 8, HD), F32),
            V((2, 4, 2, 64, HD), BF16),
            V((2, 4, 2, 64, HD), BF16),
            V((2, 4, 8, HD), F32),
            V((2, 4, 8, HD), F32),
            V((2, 3, 2, 64, HD), BF16),
            V((2, 3, 2, 64, HD), BF16),
            V((2, 3, 8, HD), F32),
            V((2, 3, 8, HD), F32),
            V((8, 64, HD), BF16),
            V((8, 1, HD), F32),
            V((7, 64, HD), BF16),
            V((7, 1, HD), F32),
            sem(9), sem(4), sem(2), sem(2), sem(3), sem(3), sem(3), sem(3),
            sem(7), sem(7), sem(2, 2, 3), sem(2, 2, 3), sem(2, 2, 3), sem(2, 2, 3),
            sem(2, 4, 3), sem(2, 4, 3), sem(2, 4, 3), sem(2, 4, 3), sem(2, 7), sem(2, 7),
        ],
        compiler_params=pltpu.CompilerParams(
            collective_id=0, has_side_effects=True, vmem_limit_bytes=60 * 1024 * 1024
        ),
    )(
        prompt_dest.reshape(-1), context_len.T, partner, mig_slot, block_table,
        prompt_dest.reshape(24, HD), jnp.asarray(rope_row()), queries, step_kv.reshape(5, 16, HD),
        pool_kv, prompt_kv,
    )


def solution(mesh):
    placed = (
        P("inst", None, "tp", None, None),
        P("inst", None),
        P(),
        P(),
        P(),
        P(("inst", "tp"), None, None, None, None),
        P(),
        P("inst", None, "tp", None),
        P("inst", None, None, "tp", None),
    )
    return jax.shard_map(
        per_device,
        mesh=mesh,
        in_specs=placed,
        out_specs=P("inst", None, "tp", None),
        check_vma=False,
    )
```

```python
import math

import jax
import jax.numpy as jnp
import numpy as np
from jax import lax
from jax.experimental import pallas as pl
from jax.experimental.pallas import tpu as pltpu
from jax.sharding import PartitionSpec as P

MESH = pl.DeviceIdType.MESH
NEG = -1e30
F32 = jnp.float32
BF16 = jnp.bfloat16
HD = 128
SCALE = 1.0 / math.sqrt(HD)
UNROLL = 3


def rope_row():
    ratio = np.arange(HD // 2) * (2.0 / HD)
    base = np.exp(-ratio * math.log(500000.0))
    wavelength = 2.0 * math.pi / base
    smooth = (8192.0 / wavelength - 1.0) / 3.0
    blended = (1.0 - smooth) * base / 8.0 + smooth * base
    freqs = np.where(wavelength < 2048.0, base, np.where(wavelength > 8192.0, base / 8.0, blended))
    return np.concatenate([freqs, freqs])[None].astype(np.float32)


def cos_sin(angle):
    turns = jnp.floor(angle * (2.0 / math.pi) + 0.5)
    r = angle - turns * 1.5703125
    r = r - turns * 4.837512969970703125e-4
    r = r - turns * 7.54978995489188216e-8
    sq = r * r
    sine = ((-1.9515295891e-4 * sq + 8.3321608736e-3) * sq - 1.6666654611e-1) * sq * r + r
    cosine = (2.443315711809948e-5 * sq - 1.388731625493765e-3) * sq + 4.166664568298827e-2
    cosine = cosine * sq * sq - 0.5 * sq + 1.0
    quarter = turns - 4.0 * jnp.floor(turns * 0.25)
    odd = (quarter == 1.0) | (quarter == 3.0)
    first, second = jnp.where(odd, sine, cosine), jnp.where(odd, cosine, sine)
    first = jnp.where((quarter == 1.0) | (quarter == 2.0), -first, first)
    second = jnp.where(quarter >= 2.0, -second, second)
    return first, second


def dot_nn(a, b):
    return lax.dot_general(a, b, (((1,), (0,)), ((), ())), preferred_element_type=F32)


def dot_tn(a, b):
    return lax.dot_general(a, b, (((0,), (0,)), ((), ())), preferred_element_type=F32)


def shares(parts):
    top = parts[0]
    for part in parts[1:]:
        top = jnp.maximum(top, part)
    weights = [jnp.exp(part - top) for part in parts]
    total = weights[0]
    for part in weights[1:]:
        total = total + part
    return [part / total for part in weights], top + jnp.log(total)


def iota(shape, axis):
    return lax.broadcasted_iota(jnp.int32, shape, axis)


def body(
    dests_in, lengths_in, partner_in, mig_slot_in, table_in, grid_in, freqs_in, queries_in, kv_in,
    pool_hbm, prompt_hbm, out,
    dests, lengths, partner, mig_slot, table, dest_grid, freqs, queries, step_kv,
    pool, pages, ab, index_v, index, mig_mine, mig_send, mig_rcv, ret_loc, ret_send, ret_rcv,
    zq, qa_low, qa_high, qb_low, qb_high, acc, lse, acc2, lse2,
    sa, sb, la, lb, ra, rb, rla, rlb,
    sa2, sb2, la2, lb2, ra2, rb2, rla2, rlb2,
    s3, l3, r3, rl3,
    in_sem, local_sem, core_ssem, core_rsem, mig_ssem, mig_rsem, ret_ssem, ret_rsem,
    gz_ssem, gz_rsem, g2_ssem, g2_rsem, g3_ssem, g3_rsem,
    r1_ssem, r1_rsem, r2_ssem, r2_rsem, rz_ssem, rz_rsem,
):
    inst = lax.axis_index("inst")
    tp = lax.axis_index("tp")
    z_lo, y, x = inst // 16, (inst // 4) % 4, inst % 4
    z_hi, core = tp // 2, tp % 2
    z = z_hi * 4 + z_lo

    def device(zz, yy, xx, cc):
        return ((zz % 4) * 16 + yy * 4 + xx, (zz // 4) * 2 + cc)

    x_peers = [device(z, y, (x + k) % 4, core) for k in (1, 2, 3)]
    y_peers = [device(z, (y + k) % 4, x, core) for k in (1, 2, 3)]
    z_peers = [device((z + k) % 8, y, x, core) for k in range(1, 8)]
    core_peer = device(z, y, x, 1 - core)
    mig_peers = [
        device(z, y, x + 1 - 2 * (x % 2), core),
        device(z, y, (x + 2) % 4, core),
        device(z, y + 1 - 2 * (y % 2), x, core),
    ]

    barrier = pltpu.get_barrier_semaphore()
    everyone = [core_peer] + x_peers + y_peers + z_peers
    for peer in everyone:
        pl.semaphore_signal(barrier, inc=1, device_id=peer, device_id_type=MESH)

    def remote(src, dst, ssem, rsem, peer):
        return pltpu.make_async_remote_copy(
            src_ref=src, dst_ref=dst, send_sem=ssem, recv_sem=rsem,
            device_id=peer, device_id_type=MESH,
        )

    inputs = [
        pltpu.make_async_copy(src, dst, in_sem.at[n])
        for n, (src, dst) in enumerate((
            (grid_in, dest_grid), (freqs_in, freqs), (queries_in, queries), (mig_slot_in, mig_slot),
            (partner_in, partner), (lengths_in, lengths), (dests_in, dests), (table_in, table), (kv_in, step_kv),
        ))
    ]
    for copy in inputs:
        copy.start()
    pool_copy = pltpu.make_async_copy(pool_hbm, pool, local_sem.at[0])
    pool_copy.start()
    own_copies = [
        pltpu.make_async_copy(
            prompt_hbm.at[:, :, pl.ds(hi * 4 + core * 2, 2)], pages.at[core, hi], local_sem.at[1 + hi]
        )
        for hi in range(2)
    ]
    for copy in own_copies:
        copy.start()

    first_row = inst * 48 + z_hi * 24

    for copy in inputs[:3]:
        copy.wait()
    freq = freqs[...]
    lane8 = iota((8, HD), 1)
    line8 = iota((8, HD), 0)
    line16 = iota((16, HD), 0)
    sign = jnp.where(lane8[:1] < 64, -1.0, 1.0)
    is_key = (line16 // 2) % 2 == 0

    def tables(length):
        at = length + (line8 % 4).astype(F32)
        cosine, sine = cos_sin(at * freq)
        return cosine, sine * sign

    def key_tables(length):
        at = jnp.where(is_key, length + (line16 // 4).astype(F32), 0.0)
        cosine, sine = cos_sin(at * freq)
        return cosine, sine * sign

    def turn(value, cosine, sine):
        return value * cosine + pltpu.roll(value, 64, 1) * sine

    def turned_query(slot, cosine, sine):
        tiles = [[None] * 4, [None] * 4]
        for s in range(4):
            both = queries[slot, s].astype(F32)
            for h in range(2):
                tiles[h][s] = turn(both[h * 8 : h * 8 + 8], cosine[s : s + 1], sine[s : s + 1])
        return [jnp.concatenate(part, axis=0) for part in tiles]

    named_here = jnp.where(dest_grid[...] == inst, 1.0, 0.0)
    new_len = jnp.sum(jnp.sum(named_here, axis=0, keepdims=True), axis=1, keepdims=True) * 64.0
    mine = turned_query(4, *tables(new_len))
    twice = jnp.concatenate(mine + mine, axis=0).T
    zq[z] = jnp.where(iota((64, HD), 1) < 64, twice[:64], twice[64:]).astype(BF16)
    twice = twice.astype(BF16)
    qa, qb = (qa_low, qa_high), (qb_low, qb_high)

    pl.semaphore_wait(barrier, len(everyone))

    gz = []
    for k in range(7):
        gz.append(remote(zq.at[z], zq.at[z], gz_ssem.at[k], gz_rsem.at[k], z_peers[k]))
    for copy in gz:
        copy.start()
    for copy in inputs[3:]:
        copy.wait()

    my_slot = mig_slot[inst]
    mate = partner[inst]
    mate_len = lengths[mig_slot[mate], mate]
    own_len = [lengths[j, inst] for j in range(4)]
    bit = jnp.where(mate // 4 != inst // 4, 2, jnp.where(mate // 2 != inst // 2, 1, 0))

    for j in range(4):
        length = jnp.where(my_slot == j, mate_len, own_len[j]).astype(F32)
        part = turned_query(j, *tables(length))
        mig_mine[j, pl.ds(0, 32)] = part[0].astype(BF16)
        mig_mine[j, pl.ds(32, 32)] = part[1].astype(BF16)
        mig_mine[j, pl.ds(64, 16)] = turn(step_kv[j].astype(F32), *key_tables(length)).astype(BF16)
    mig_send[...] = mig_mine[my_slot]
    mig = [remote(mig_send, mig_rcv.at[k], mig_ssem.at[k], mig_rsem.at[k], mig_peers[k]) for k in range(3)]
    for copy in mig:
        copy.start()
    core_copies = [
        remote(
            prompt_hbm.at[:, :, pl.ds(hi * 4 + (1 - core) * 2, 2)],
            pages.at[core, hi], core_ssem.at[hi], core_rsem.at[hi], core_peer,
        )
        for hi in range(2)
    ]
    for copy in core_copies:
        copy.start()

    first = jnp.full((8, HD), 24, jnp.int32)
    second = jnp.full((8, HD), 24, jnp.int32)
    for n in range(24):
        hit = lane8 == dests[first_row + n]
        second = jnp.where(hit & (first < 24), n, second)
        first = jnp.where(hit & (first == 24), n, first)
    index_v[...] = jnp.where(line8 == 0, first, second)
    index_copy = pltpu.make_async_copy(index_v, index, local_sem.at[3])
    index_copy.start()

    own_kv = turn(step_kv[4].astype(F32), *key_tables(new_len)).astype(BF16)
    lane16 = iota((16, HD), 1)
    ok = is_key & (line16 % 2 == (lane16 % 64) // 32) & (line16 // 4 <= (lane16 % 32) // 8)
    score = jnp.where(ok, dot_nn(own_kv, twice) * SCALE, NEG)
    top = jnp.max(score, axis=0, keepdims=True)
    weight = jnp.where(ok, jnp.exp(score - top), 0.0).astype(BF16).astype(F32)
    total = jnp.sum(weight, axis=0, keepdims=True)
    new_acc = dot_tn(own_kv, pltpu.roll(weight, 2, 0).astype(BF16)) / total
    new_acc = jnp.where(iota((64, HD), 1) < 64, new_acc[:64], new_acc[64:])
    new_lse = top + jnp.log(total)

    for copy in gz:
        copy.wait_recv()
    g2 = [[], []]
    for hi in range(2):
        part = zq.at[pl.ds(hi * 4, 4), pl.ds(0, 32)]
        other = zq.at[pl.ds(hi * 4, 4), pl.ds(32, 32)]
        for k in range(3):
            g2[hi].append(remote(part, qa[hi].at[x, y], g2_ssem.at[hi, 0, k], g2_rsem.at[hi, 0, k], y_peers[k]))
            g2[hi].append(remote(other, qb[hi].at[y, x], g2_ssem.at[hi, 1, k], g2_rsem.at[hi, 1, k], x_peers[k]))
        for copy in g2[hi]:
            copy.start()
    for hi in range(2):
        qa[hi][x, y] = zq[pl.ds(hi * 4, 4), pl.ds(0, 32)]
        qb[hi][y, x] = zq[pl.ds(hi * 4, 4), pl.ds(32, 32)]
    shape = (12, 8, HD)
    row = iota(shape, 1)
    page_id = iota(shape, 0) * 4 + row % 4
    is_last = row // 4
    lane1 = lane8[:1]

    def by_slot(values):
        return jnp.where(
            lane1 < 64, jnp.where(lane1 < 32, values[0], values[1]), jnp.where(lane1 < 96, values[2], values[3])
        )

    context = by_slot(own_len)
    full, rem = context // 64, context % 64
    ab[...] = jnp.zeros(shape, F32)

    def count_step(k, carry):
        named = by_slot([table[j, k] for j in range(4)])[None]
        kind = jnp.where(k < full, 0, jnp.where(k == full, 1, 2))[None]
        hit = (page_id == named) & (is_last == kind)
        ab[...] += jnp.where(hit, 1.0, 0.0)
        return carry

    lax.fori_loop(0, 24, count_step, 0)

    for copy in mig:
        copy.wait_recv()

    came = mig_rcv[bit].astype(F32)
    blocks = [jnp.where(my_slot == j, came, mig_mine[j].astype(F32)) for j in range(4)]
    fresh_kv = jnp.concatenate([block[64:80] for block in blocks], axis=0).astype(BF16)
    q_res = [
        jnp.concatenate([block[h * 32 : h * 32 + 32] for block in blocks], axis=0).T.astype(BF16) for h in range(2)
    ]
    pool_copy.wait()
    below = (iota((64, HD), 0) < rem).astype(F32)

    def res_step(i, carry):
        named = [ab[i * 2 + n] for n in range(2)]
        count = jnp.concatenate(
            [(part[0:4][:, None, :] + part[4:8][:, None, :] * below[None]).reshape(256, HD) for part in named], axis=0
        )
        real = count > 0.0
        after = []
        for h in range(2):
            best, total, summed = carry[3 * h : 3 * h + 3]
            keys = pool[pl.ds(i * 8, 8), 0, h].reshape(512, HD)
            values = pool[pl.ds(i * 8, 8), 1, h].reshape(512, HD)
            score = jnp.where(real, dot_nn(keys, q_res[h]) * SCALE, NEG)
            top = jnp.maximum(best, jnp.max(score, axis=0, keepdims=True))
            weight = (count * jnp.exp(score - top)).astype(BF16)
            shrink = jnp.exp(best - top)
            total = total * shrink + jnp.sum(weight.astype(F32), axis=0, keepdims=True)
            summed = summed * shrink + dot_tn(values, weight)
            after += [top, total, summed]
        return tuple(after)

    start = (jnp.full((1, HD), NEG, F32), jnp.zeros((1, HD), F32), jnp.zeros((HD, HD), F32)) * 2
    state = lax.fori_loop(0, 2, res_step, start)
    right = ((x + 1) % 4, (y + 1) % 4)
    left_by = ((x + 3) % 4, (y + 3) % 4)
    right_peer, left_peer = (x_peers[0], y_peers[0]), (x_peers[2], y_peers[2])
    place = (x, y)

    def ring(hi, side, kind, row, peer):
        part = (qa, qb)[side][hi].at[row]
        return remote(part, part, g3_ssem.at[hi, side, kind], g3_rsem.at[hi, side, kind], peer)

    g3 = [
        [[ring(hi, side, 0, place[side], right_peer[side]) for side in range(2)],
         [ring(hi, side, 1, place[side], left_peer[side]) for side in range(2)],
         [ring(hi, side, 2, (left_by, right)[hi][side], (right_peer, left_peer)[hi][side]) for side in range(2)]]
        for hi in range(2)
    ]
    for copy in g2[0]:
        copy.wait_recv()
    for copy in g3[0][0] + g3[0][1]:
        copy.start()
    for copy in g2[1]:
        copy.wait_recv()
    for copy in g3[1][1]:
        copy.start()
    state = lax.fori_loop(2, 4, res_step, state)
    for copy in g3[0][0]:
        copy.wait_recv()
    for copy in g3[0][2]:
        copy.start()
    state = lax.fori_loop(4, 6, res_step, state)
    lane = iota((64, HD), 1)
    line = iota((64, HD), 0)
    ok_slot = (line // 16 == lane // 32) & ((line // 2) % 2 == 0) & ((line % 16) // 4 <= (lane % 32) // 8)
    rows = []
    for h in range(2):
        best, total, summed = state[3 * h : 3 * h + 3]
        ok = ok_slot & (line % 2 == h)
        score = jnp.where(ok, dot_nn(fresh_kv, q_res[h]) * SCALE, NEG)
        top = jnp.maximum(best, jnp.max(score, axis=0, keepdims=True))
        weight = jnp.where(ok, jnp.exp(score - top), 0.0).astype(BF16).astype(F32)
        shrink = jnp.exp(best - top)
        total = total * shrink + jnp.sum(weight, axis=0, keepdims=True)
        summed = summed * shrink + dot_tn(fresh_kv, pltpu.roll(weight, 2, 0).astype(BF16))
        rows.append((summed / total).T)
    for j in range(4):
        for s in range(4):
            at = j * 32 + s * 8
            ret_loc[j, s] = jnp.concatenate([rows[0][at : at + 8], rows[1][at : at + 8]], axis=0).astype(BF16)
    ret_send[...] = ret_loc[my_slot]
    ret = [remote(ret_send, ret_rcv.at[k], ret_ssem.at[k], ret_rsem.at[k], mig_peers[k]) for k in range(3)]
    for copy in ret:
        copy.start()

    for copy in g3[1][1]:
        copy.wait_recv()
    for copy in g3[1][2] + g3[1][0]:
        copy.start()

    for copy in own_copies:
        copy.wait()
    for copy in core_copies:
        copy.wait_recv()
    index_copy.wait()
    acc[24] = jnp.zeros((HD, HD), F32)
    acc2[24] = jnp.zeros((HD, HD), F32)
    lse[24] = jnp.full((1, HD), NEG, F32)
    lse2[24] = jnp.full((1, HD), NEG, F32)
    same_head = iota((HD, HD), 0) // 64 == (iota((HD, HD), 1) % 64) // 32
    left = iota((HD, HD), 1) < 64
    left1 = lane1 < 64
    left64 = lane < 64
    zeros6 = jnp.zeros((6, HD), F32)

    def prompt_part(hi):
        def page(n, src, i):
            d = dests[first_row + n]
            zl, dy, dx = d // 16, (d // 4) % 4, d % 4
            part = jnp.concatenate([qa[hi][dx, dy, zl], qb[hi][dy, dx, zl]], axis=0)
            swap = jnp.concatenate([part[:, 64:], part[:, :64]], axis=1)
            asked = jnp.concatenate([jnp.where(left64, part, swap), jnp.where(left64, swap, part)], axis=0)
            score = jnp.where(same_head, dot_nn(pages[src, hi, i, 0].reshape(HD, HD), asked) * SCALE, NEG)
            top = jnp.max(score, axis=0, keepdims=True)
            weight = jnp.exp(score - top).astype(BF16)
            total = jnp.sum(weight.astype(F32), axis=0, keepdims=True)
            acc[n] = dot_tn(pages[src, hi, i, 1].reshape(HD, HD), weight) / total
            lse[n] = top + jnp.log(total)

        def page_step(i, carry):
            for src in range(2):
                for more in range(UNROLL):
                    page(src * 12 + i * UNROLL + more, src, i * UNROLL + more)
            return carry

        lax.fori_loop(0, 12 // UNROLL, page_step, 0)

        def join_step(i, carry):
            for more in range(4):
                n = i * 4 + more
                d = dests[first_row + n]
                first = index[0, d]
                other = jnp.where(first == n, index[1, d], first)
                weights, joined = shares([lse[n], lse[other]])
                acc2[n] = acc[n] * weights[0] + acc[other] * weights[1]
                lse2[n] = joined
            return carry

        lax.fori_loop(0, 6, join_step, 0)

        for zp in range(2):
            def place_step(dy, carry):
                for dx in range(4):
                    d = zp * 32 + dy * 4 + dx
                    one, two = index[0, d], index[0, d + 16]
                    block = jnp.where(left, acc2[one], acc2[two]).astype(BF16)
                    stat = jnp.where(left1, lse2[one], lse2[two])
                    sa[hi, dx, dy * 2 + zp] = block[:64]
                    sb[hi, dy, dx * 2 + zp] = block[64:]
                    la[hi, dx, pl.ds(dy * 2 + zp, 1), :] = stat
                    lb[hi, dy, pl.ds(dx * 2 + zp, 1), :] = stat
                return carry

            lax.fori_loop(0, 4, place_step, 0)

    def send_first(hi):
        sent = []
        for k in range(3):
            to_x, to_y = (x + k + 1) % 4, (y + k + 1) % 4
            for m, (src, dst, peer) in enumerate((
                (sa.at[hi, to_x], ra.at[hi, k], x_peers[k]),
                (sb.at[hi, to_y], rb.at[hi, k], y_peers[k]),
                (la.at[hi, to_x], rla.at[hi, k], x_peers[k]),
                (lb.at[hi, to_y], rlb.at[hi, k], y_peers[k]),
            )):
                sent.append(remote(src, dst, r1_ssem.at[hi, m, k], r1_rsem.at[hi, m, k], peer))
        for copy in sent:
            copy.start()
        return sent

    def merge_first(hi):
        for mine_s, mine_l, got_s, got_l, where, next_s, next_l in (
            (sa, la, ra, rla, x, sa2, la2), (sb, lb, rb, rlb, y, sb2, lb2)
        ):
            weights, joined = shares([mine_l[hi, where]] + [got_l[hi, k] for k in range(3)])
            for t in range(8):
                block = mine_s[hi, where, t].astype(F32) * weights[0][t : t + 1]
                for k in range(3):
                    block = block + got_s[hi, k, t].astype(F32) * weights[k + 1][t : t + 1]
                next_s[hi, t // 2, t % 2] = block.astype(BF16)
            for group in range(4):
                next_l[hi, group] = jnp.concatenate([joined[group * 2 : group * 2 + 2], zeros6], axis=0)

    def send_second(hi):
        sent = []
        for k in range(3):
            to_x, to_y = (x + k + 1) % 4, (y + k + 1) % 4
            for m, (src, dst, peer) in enumerate((
                (sa2.at[hi, to_y], ra2.at[hi, k], y_peers[k]),
                (sb2.at[hi, to_x], rb2.at[hi, k], x_peers[k]),
                (la2.at[hi, to_y], rla2.at[hi, k], y_peers[k]),
                (lb2.at[hi, to_x], rlb2.at[hi, k], x_peers[k]),
            )):
                sent.append(remote(src, dst, r2_ssem.at[hi, m, k], r2_rsem.at[hi, m, k], peer))
        for copy in sent:
            copy.start()
        return sent

    def merge_second(hi):
        both = []
        for mine_s, mine_l, got_s, got_l, where in ((sa2, la2, ra2, rla2, y), (sb2, lb2, rb2, rlb2, x)):
            weights, joined = shares([mine_l[hi, where]] + [got_l[hi, k] for k in range(3)])
            blocks = []
            for zp in range(2):
                block = mine_s[hi, where, zp].astype(F32) * weights[0][zp : zp + 1]
                for k in range(3):
                    block = block + got_s[hi, k, zp].astype(F32) * weights[k + 1][zp : zp + 1]
                blocks.append(block)
            both.append((blocks, joined))
        for zp in range(2):
            a, b = both[0][0][zp], both[1][0][zp]
            s3[hi * 4 + zp * 2] = jnp.where(left64, a, pltpu.roll(b, 64, 1)).astype(BF16)
            s3[hi * 4 + zp * 2 + 1] = jnp.where(left64, pltpu.roll(a, 64, 1), b).astype(BF16)
            a, b = both[0][1], both[1][1]
            l3[hi * 4 + zp * 2] = jnp.where(lane8 < 64, a, pltpu.roll(b, 64, 1))[zp : zp + 1]
            l3[hi * 4 + zp * 2 + 1] = jnp.where(lane8 < 64, pltpu.roll(a, 64, 1), b)[zp : zp + 1]

    for copy in g3[0][1] + g3[0][2]:
        copy.wait_recv()
    prompt_part(0)
    r1_low = send_first(0)
    for copy in g3[1][0] + g3[1][2]:
        copy.wait_recv()
    prompt_part(1)
    r1_high = send_first(1)
    for copy in gz + g2[0] + g2[1] + g3[0][0] + g3[0][1] + g3[0][2] + g3[1][0] + g3[1][1] + g3[1][2] + mig + core_copies:
        copy.wait_send()
    for copy in ret:
        copy.wait_recv()
    back = [ret_rcv[bit, s].astype(F32) for s in range(4)]
    for j in range(4):
        for s in range(4):
            out[j, s] = jnp.where(my_slot == j, back[s], ret_loc[j, s].astype(F32)).astype(BF16)
    for copy in r1_low:
        copy.wait_recv()
    merge_first(0)
    r2_low = send_second(0)
    for copy in r1_high:
        copy.wait_recv()
    merge_first(1)
    r2_high = send_second(1)
    for copy in r2_low:
        copy.wait_recv()
    merge_second(0)
    for copy in r2_high:
        copy.wait_recv()
    merge_second(1)

    rz = []
    for k in range(7):
        to = (z + k + 1) % 8
        rz.append(remote(s3.at[to], r3.at[k], rz_ssem.at[0, k], rz_rsem.at[0, k], z_peers[k]))
        rz.append(remote(l3.at[to], rl3.at[k], rz_ssem.at[1, k], rz_rsem.at[1, k], z_peers[k]))
    for copy in rz:
        copy.start()
    for copy in r1_low + r1_high + r2_low + r2_high + ret:
        copy.wait_send()
    for copy in rz:
        copy.wait_recv()
    weights, _ = shares([new_lse, l3[z]] + [rl3[k] for k in range(7)])
    block = new_acc * weights[0] + s3[z].astype(F32) * weights[1]
    for k in range(7):
        block = block + r3[k].astype(F32) * weights[k + 2]
    flat = jnp.concatenate([block, block], axis=0).T
    here = jnp.where(left64, flat[:64], flat[64:])
    for s in range(4):
        out[4, s] = jnp.concatenate([here[s * 8 : s * 8 + 8], here[32 + s * 8 : 40 + s * 8]], axis=0).astype(BF16)
    for copy in rz:
        copy.wait_send()


def per_device(
    pool_kv, block_table, context_len, partner, mig_slot, prompt_kv, prompt_dest, queries, step_kv
):
    vmem = pl.BlockSpec(memory_space=pltpu.VMEM)
    hbm = pl.BlockSpec(memory_space=pltpu.HBM)
    sem = lambda *shape: pltpu.SemaphoreType.DMA(shape)
    V = pltpu.VMEM
    return pl.pallas_call(
        body,
        out_shape=jax.ShapeDtypeStruct((5, 4, 16, HD), BF16),
        in_specs=[hbm] * 11,
        out_specs=vmem,
        scratch_shapes=[
            pltpu.SMEM((3072,), jnp.int32),
            pltpu.SMEM((4, 64), jnp.int32),
            pltpu.SMEM((64,), jnp.int32),
            pltpu.SMEM((64,), jnp.int32),
            pltpu.SMEM((4, 24), jnp.int32),
            V((24, HD), jnp.int32),
            V((1, HD), F32),
            V((5, 4, 16, HD), BF16),
            V((5, 16, HD), BF16),
            V((48, 2, 2, 64, HD), BF16),
            V((2, 2, 12, 2, 2, 64, HD), BF16),
            V((12, 8, HD), F32),
            V((8, HD), jnp.int32),
            pltpu.SMEM((8, HD), jnp.int32),
            V((4, 80, HD), BF16),
            V((80, HD), BF16),
            V((3, 80, HD), BF16),
            V((4, 4, 16, HD), BF16),
            V((4, 16, HD), BF16),
            V((3, 4, 16, HD), BF16),
            V((8, 64, HD), BF16),
            V((4, 4, 4, 32, HD), BF16),
            V((4, 4, 4, 32, HD), BF16),
            V((4, 4, 4, 32, HD), BF16),
            V((4, 4, 4, 32, HD), BF16),
            V((25, HD, HD), F32),
            V((25, 1, HD), F32),
            V((25, HD, HD), F32),
            V((25, 1, HD), F32),
            V((2, 4, 8, 64, HD), BF16),
            V((2, 4, 8, 64, HD), BF16),
            V((2, 4, 8, HD), F32),
            V((2, 4, 8, HD), F32),
            V((2, 3, 8, 64, HD), BF16),
            V((2, 3, 8, 64, HD), BF16),
            V((2, 3, 8, HD), F32),
            V((2, 3, 8, HD), F32),
            V((2, 4, 2, 64, HD), BF16),
            V((2, 4, 2, 64, HD), BF16),
            V((2, 4, 8, HD), F32),
            V((2, 4, 8, HD), F32),
            V((2, 3, 2, 64, HD), BF16),
            V((2, 3, 2, 64, HD), BF16),
            V((2, 3, 8, HD), F32),
            V((2, 3, 8, HD), F32),
            V((8, 64, HD), BF16),
            V((8, 1, HD), F32),
            V((7, 64, HD), BF16),
            V((7, 1, HD), F32),
            sem(9), sem(4), sem(2), sem(2), sem(3), sem(3), sem(3), sem(3),
            sem(7), sem(7), sem(2, 2, 3), sem(2, 2, 3), sem(2, 2, 3), sem(2, 2, 3),
            sem(2, 4, 3), sem(2, 4, 3), sem(2, 4, 3), sem(2, 4, 3), sem(2, 7), sem(2, 7),
        ],
        compiler_params=pltpu.CompilerParams(
            collective_id=0, has_side_effects=True, vmem_limit_bytes=60 * 1024 * 1024
        ),
    )(
        prompt_dest.reshape(-1), context_len.T, partner, mig_slot, block_table,
        prompt_dest.reshape(24, HD), jnp.asarray(rope_row()), queries, step_kv.reshape(5, 16, HD),
        pool_kv, prompt_kv,
    )


def solution(mesh):
    placed = (
        P("inst", None, "tp", None, None),
        P("inst", None),
        P(),
        P(),
        P(),
        P(("inst", "tp"), None, None, None, None),
        P(),
        P("inst", None, "tp", None),
        P("inst", None, None, "tp", None),
    )
    return jax.shard_map(
        per_device,
        mesh=mesh,
        in_specs=placed,
        out_specs=P("inst", None, "tp", None),
        check_vma=False,
    )
```

```python
import math

import jax
import jax.numpy as jnp
import numpy as np
from jax import lax
from jax.experimental import pallas as pl
from jax.experimental.pallas import tpu as pltpu
from jax.sharding import PartitionSpec as P

MESH = pl.DeviceIdType.MESH
NEG = -1e30
F32 = jnp.float32
BF16 = jnp.bfloat16
HD = 128
SCALE = 1.0 / math.sqrt(HD)
UNROLL = 3


def rope_row():
    ratio = np.arange(HD // 2) * (2.0 / HD)
    base = np.exp(-ratio * math.log(500000.0))
    wavelength = 2.0 * math.pi / base
    smooth = (8192.0 / wavelength - 1.0) / 3.0
    blended = (1.0 - smooth) * base / 8.0 + smooth * base
    freqs = np.where(wavelength < 2048.0, base, np.where(wavelength > 8192.0, base / 8.0, blended))
    return np.concatenate([freqs, freqs])[None].astype(np.float32)


def cos_sin(angle):
    turns = jnp.floor(angle * (2.0 / math.pi) + 0.5)
    r = angle - turns * 1.5703125
    r = r - turns * 4.837512969970703125e-4
    r = r - turns * 7.54978995489188216e-8
    sq = r * r
    sine = ((-1.9515295891e-4 * sq + 8.3321608736e-3) * sq - 1.6666654611e-1) * sq * r + r
    cosine = (2.443315711809948e-5 * sq - 1.388731625493765e-3) * sq + 4.166664568298827e-2
    cosine = cosine * sq * sq - 0.5 * sq + 1.0
    quarter = turns - 4.0 * jnp.floor(turns * 0.25)
    odd = (quarter == 1.0) | (quarter == 3.0)
    first, second = jnp.where(odd, sine, cosine), jnp.where(odd, cosine, sine)
    first = jnp.where((quarter == 1.0) | (quarter == 2.0), -first, first)
    second = jnp.where(quarter >= 2.0, -second, second)
    return first, second


def dot_nn(a, b):
    return lax.dot_general(a, b, (((1,), (0,)), ((), ())), preferred_element_type=F32)


def dot_tn(a, b):
    return lax.dot_general(a, b, (((0,), (0,)), ((), ())), preferred_element_type=F32)


def shares(parts):
    top = parts[0]
    for part in parts[1:]:
        top = jnp.maximum(top, part)
    weights = [jnp.exp(part - top) for part in parts]
    total = weights[0]
    for part in weights[1:]:
        total = total + part
    return [part / total for part in weights], top + jnp.log(total)


def iota(shape, axis):
    return lax.broadcasted_iota(jnp.int32, shape, axis)


def body(
    dests_in, lengths_in, partner_in, mig_slot_in, table_in, grid_in, freqs_in, queries_in, kv_in,
    pool_hbm, prompt_hbm, out,
    dests, lengths, partner, mig_slot, table, dest_grid, freqs, queries, step_kv,
    pool, pages, ab, index_v, index, mig_mine, mig_send, mig_rcv, ret_loc, ret_send, ret_rcv,
    zq, qa_low, qa_high, qb_low, qb_high, acc, lse, acc2, lse2,
    sa, sb, la, lb, ra, rb, rla, rlb,
    sa2, sb2, la2, lb2, ra2, rb2, rla2, rlb2,
    s3, l3, r3, rl3,
    in_sem, local_sem, core_ssem, core_rsem, mig_ssem, mig_rsem, ret_ssem, ret_rsem,
    gz_ssem, gz_rsem, g2_ssem, g2_rsem, g3_ssem, g3_rsem,
    r1_ssem, r1_rsem, r2_ssem, r2_rsem, rz_ssem, rz_rsem,
):
    inst = lax.axis_index("inst")
    tp = lax.axis_index("tp")
    z_lo, y, x = inst // 16, (inst // 4) % 4, inst % 4
    z_hi, core = tp // 2, tp % 2
    z = z_hi * 4 + z_lo

    def device(zz, yy, xx, cc):
        return ((zz % 4) * 16 + yy * 4 + xx, (zz // 4) * 2 + cc)

    x_peers = [device(z, y, (x + k) % 4, core) for k in (1, 2, 3)]
    y_peers = [device(z, (y + k) % 4, x, core) for k in (1, 2, 3)]
    z_peers = [device((z + k) % 8, y, x, core) for k in range(1, 8)]
    core_peer = device(z, y, x, 1 - core)
    mig_peers = [
        device(z, y, x + 1 - 2 * (x % 2), core),
        device(z, y, (x + 2) % 4, core),
        device(z, y + 1 - 2 * (y % 2), x, core),
    ]

    barrier = pltpu.get_barrier_semaphore()
    everyone = [core_peer] + x_peers + y_peers + z_peers
    for peer in everyone:
        pl.semaphore_signal(barrier, inc=1, device_id=peer, device_id_type=MESH)

    def remote(src, dst, ssem, rsem, peer):
        return pltpu.make_async_remote_copy(
            src_ref=src, dst_ref=dst, send_sem=ssem, recv_sem=rsem,
            device_id=peer, device_id_type=MESH,
        )

    inputs = [
        pltpu.make_async_copy(src, dst, in_sem.at[n])
        for n, (src, dst) in enumerate((
            (grid_in, dest_grid), (freqs_in, freqs), (queries_in, queries), (mig_slot_in, mig_slot),
            (partner_in, partner), (lengths_in, lengths), (dests_in, dests), (table_in, table), (kv_in, step_kv),
        ))
    ]
    for copy in inputs:
        copy.start()
    pool_copy = pltpu.make_async_copy(pool_hbm, pool, local_sem.at[0])
    pool_copy.start()
    own_copies = [
        pltpu.make_async_copy(
            prompt_hbm.at[:, :, pl.ds(hi * 4 + core * 2, 2)], pages.at[core, hi], local_sem.at[1 + hi]
        )
        for hi in range(2)
    ]
    for copy in own_copies:
        copy.start()

    first_row = inst * 48 + z_hi * 24

    for copy in inputs[:3]:
        copy.wait()
    freq = freqs[...]
    lane8 = iota((8, HD), 1)
    line8 = iota((8, HD), 0)
    line16 = iota((16, HD), 0)
    sign = jnp.where(lane8[:1] < 64, -1.0, 1.0)
    is_key = (line16 // 2) % 2 == 0

    def tables(length):
        at = length + (line8 % 4).astype(F32)
        cosine, sine = cos_sin(at * freq)
        return cosine, sine * sign

    def key_tables(length):
        at = jnp.where(is_key, length + (line16 // 4).astype(F32), 0.0)
        cosine, sine = cos_sin(at * freq)
        return cosine, sine * sign

    def turn(value, cosine, sine):
        return value * cosine + pltpu.roll(value, 64, 1) * sine

    def turned_query(slot, cosine, sine):
        tiles = [[None] * 4, [None] * 4]
        for s in range(4):
            both = queries[slot, s].astype(F32)
            for h in range(2):
                tiles[h][s] = turn(both[h * 8 : h * 8 + 8], cosine[s : s + 1], sine[s : s + 1])
        return [jnp.concatenate(part, axis=0) for part in tiles]

    named_here = jnp.where(dest_grid[...] == inst, 1.0, 0.0)
    new_len = jnp.sum(jnp.sum(named_here, axis=0, keepdims=True), axis=1, keepdims=True) * 64.0
    mine = turned_query(4, *tables(new_len))
    twice = jnp.concatenate(mine + mine, axis=0).T
    zq[z] = jnp.where(iota((64, HD), 1) < 64, twice[:64], twice[64:]).astype(BF16)
    twice = twice.astype(BF16)
    qa, qb = (qa_low, qa_high), (qb_low, qb_high)

    pl.semaphore_wait(barrier, len(everyone))

    gz = []
    for k in (3, 2, 4, 1, 5, 0, 6):
        gz.append(remote(zq.at[z], zq.at[z], gz_ssem.at[k], gz_rsem.at[k], z_peers[k]))
    for copy in gz:
        copy.start()
    for copy in inputs[3:]:
        copy.wait()

    my_slot = mig_slot[inst]
    mate = partner[inst]
    mate_len = lengths[mig_slot[mate], mate]
    own_len = [lengths[j, inst] for j in range(4)]
    bit = jnp.where(mate // 4 != inst // 4, 2, jnp.where(mate // 2 != inst // 2, 1, 0))

    for j in range(4):
        length = jnp.where(my_slot == j, mate_len, own_len[j]).astype(F32)
        part = turned_query(j, *tables(length))
        mig_mine[j, pl.ds(0, 32)] = part[0].astype(BF16)
        mig_mine[j, pl.ds(32, 32)] = part[1].astype(BF16)
        mig_mine[j, pl.ds(64, 16)] = turn(step_kv[j].astype(F32), *key_tables(length)).astype(BF16)
    mig_send[...] = mig_mine[my_slot]
    mig = [remote(mig_send, mig_rcv.at[k], mig_ssem.at[k], mig_rsem.at[k], mig_peers[k]) for k in range(3)]
    for copy in mig:
        copy.start()
    core_copies = [
        remote(
            prompt_hbm.at[:, :, pl.ds(hi * 4 + (1 - core) * 2, 2)],
            pages.at[core, hi], core_ssem.at[hi], core_rsem.at[hi], core_peer,
        )
        for hi in range(2)
    ]
    for copy in core_copies:
        copy.start()

    first = jnp.full((8, HD), 24, jnp.int32)
    second = jnp.full((8, HD), 24, jnp.int32)
    for n in range(24):
        hit = lane8 == dests[first_row + n]
        second = jnp.where(hit & (first < 24), n, second)
        first = jnp.where(hit & (first == 24), n, first)
    index_v[...] = jnp.where(line8 == 0, first, second)
    index_copy = pltpu.make_async_copy(index_v, index, local_sem.at[3])
    index_copy.start()

    own_kv = turn(step_kv[4].astype(F32), *key_tables(new_len)).astype(BF16)
    lane16 = iota((16, HD), 1)
    ok = is_key & (line16 % 2 == (lane16 % 64) // 32) & (line16 // 4 <= (lane16 % 32) // 8)
    score = jnp.where(ok, dot_nn(own_kv, twice) * SCALE, NEG)
    top = jnp.max(score, axis=0, keepdims=True)
    weight = jnp.where(ok, jnp.exp(score - top), 0.0).astype(BF16).astype(F32)
    total = jnp.sum(weight, axis=0, keepdims=True)
    new_acc = dot_tn(own_kv, pltpu.roll(weight, 2, 0).astype(BF16)) / total
    new_acc = jnp.where(iota((64, HD), 1) < 64, new_acc[:64], new_acc[64:])
    new_lse = top + jnp.log(total)

    for copy in gz:
        copy.wait_recv()
    g2 = [[], []]
    for hi in range(2):
        part = zq.at[pl.ds(hi * 4, 4), pl.ds(0, 32)]
        other = zq.at[pl.ds(hi * 4, 4), pl.ds(32, 32)]
        for k in range(3):
            g2[hi].append(remote(part, qa[hi].at[x, y], g2_ssem.at[hi, 0, k], g2_rsem.at[hi, 0, k], y_peers[k]))
            g2[hi].append(remote(other, qb[hi].at[y, x], g2_ssem.at[hi, 1, k], g2_rsem.at[hi, 1, k], x_peers[k]))
        for copy in g2[hi]:
            copy.start()
    for hi in range(2):
        qa[hi][x, y] = zq[pl.ds(hi * 4, 4), pl.ds(0, 32)]
        qb[hi][y, x] = zq[pl.ds(hi * 4, 4), pl.ds(32, 32)]
    shape = (12, 8, HD)
    row = iota(shape, 1)
    page_id = iota(shape, 0) * 4 + row % 4
    is_last = row // 4
    lane1 = lane8[:1]

    def by_slot(values):
        return jnp.where(
            lane1 < 64, jnp.where(lane1 < 32, values[0], values[1]), jnp.where(lane1 < 96, values[2], values[3])
        )

    context = by_slot(own_len)
    full, rem = context // 64, context % 64
    ab[...] = jnp.zeros(shape, F32)

    def count_step(k, carry):
        named = by_slot([table[j, k] for j in range(4)])[None]
        kind = jnp.where(k < full, 0, jnp.where(k == full, 1, 2))[None]
        hit = (page_id == named) & (is_last == kind)
        ab[...] += jnp.where(hit, 1.0, 0.0)
        return carry

    lax.fori_loop(0, 24, count_step, 0)

    for copy in mig:
        copy.wait_recv()

    came = mig_rcv[bit].astype(F32)
    blocks = [jnp.where(my_slot == j, came, mig_mine[j].astype(F32)) for j in range(4)]
    fresh_kv = jnp.concatenate([block[64:80] for block in blocks], axis=0).astype(BF16)
    q_res = [
        jnp.concatenate([block[h * 32 : h * 32 + 32] for block in blocks], axis=0).T.astype(BF16) for h in range(2)
    ]
    pool_copy.wait()
    below = (iota((64, HD), 0) < rem).astype(F32)

    def res_step(i, carry):
        named = [ab[i * 2 + n] for n in range(2)]
        count = jnp.concatenate(
            [(part[0:4][:, None, :] + part[4:8][:, None, :] * below[None]).reshape(256, HD) for part in named], axis=0
        )
        real = count > 0.0
        after = []
        for h in range(2):
            best, total, summed = carry[3 * h : 3 * h + 3]
            keys = pool[pl.ds(i * 8, 8), 0, h].reshape(512, HD)
            values = pool[pl.ds(i * 8, 8), 1, h].reshape(512, HD)
            score = jnp.where(real, dot_nn(keys, q_res[h]) * SCALE, NEG)
            top = jnp.maximum(best, jnp.max(score, axis=0, keepdims=True))
            weight = (count * jnp.exp(score - top)).astype(BF16)
            shrink = jnp.exp(best - top)
            total = total * shrink + jnp.sum(weight.astype(F32), axis=0, keepdims=True)
            summed = summed * shrink + dot_tn(values, weight)
            after += [top, total, summed]
        return tuple(after)

    start = (jnp.full((1, HD), NEG, F32), jnp.zeros((1, HD), F32), jnp.zeros((HD, HD), F32)) * 2
    state = lax.fori_loop(0, 2, res_step, start)
    right = ((x + 1) % 4, (y + 1) % 4)
    left_by = ((x + 3) % 4, (y + 3) % 4)
    right_peer, left_peer = (x_peers[0], y_peers[0]), (x_peers[2], y_peers[2])
    place = (x, y)

    def ring(hi, side, kind, row, peer):
        part = (qa, qb)[side][hi].at[row]
        return remote(part, part, g3_ssem.at[hi, side, kind], g3_rsem.at[hi, side, kind], peer)

    g3 = [
        [[ring(hi, side, 0, place[side], right_peer[side]) for side in range(2)],
         [ring(hi, side, 1, place[side], left_peer[side]) for side in range(2)],
         [ring(hi, side, 2, (left_by, right)[hi][side], (right_peer, left_peer)[hi][side]) for side in range(2)]]
        for hi in range(2)
    ]
    for copy in g2[0]:
        copy.wait_recv()
    for copy in g3[0][0] + g3[0][1]:
        copy.start()
    for copy in g2[1]:
        copy.wait_recv()
    for copy in g3[1][1]:
        copy.start()
    state = lax.fori_loop(2, 4, res_step, state)
    for copy in g3[0][0]:
        copy.wait_recv()
    for copy in g3[0][2]:
        copy.start()
    state = lax.fori_loop(4, 6, res_step, state)
    lane = iota((64, HD), 1)
    line = iota((64, HD), 0)
    ok_slot = (line // 16 == lane // 32) & ((line // 2) % 2 == 0) & ((line % 16) // 4 <= (lane % 32) // 8)
    rows = []
    for h in range(2):
        best, total, summed = state[3 * h : 3 * h + 3]
        ok = ok_slot & (line % 2 == h)
        score = jnp.where(ok, dot_nn(fresh_kv, q_res[h]) * SCALE, NEG)
        top = jnp.maximum(best, jnp.max(score, axis=0, keepdims=True))
        weight = jnp.where(ok, jnp.exp(score - top), 0.0).astype(BF16).astype(F32)
        shrink = jnp.exp(best - top)
        total = total * shrink + jnp.sum(weight, axis=0, keepdims=True)
        summed = summed * shrink + dot_tn(fresh_kv, pltpu.roll(weight, 2, 0).astype(BF16))
        rows.append((summed / total).T)
    for j in range(4):
        for s in range(4):
            at = j * 32 + s * 8
            ret_loc[j, s] = jnp.concatenate([rows[0][at : at + 8], rows[1][at : at + 8]], axis=0).astype(BF16)
    ret_send[...] = ret_loc[my_slot]
    ret = [remote(ret_send, ret_rcv.at[k], ret_ssem.at[k], ret_rsem.at[k], mig_peers[k]) for k in range(3)]
    for copy in ret:
        copy.start()

    for copy in g3[1][1]:
        copy.wait_recv()
    for copy in g3[1][2] + g3[1][0]:
        copy.start()

    for copy in own_copies:
        copy.wait()
    for copy in core_copies:
        copy.wait_recv()
    index_copy.wait()
    acc[24] = jnp.zeros((HD, HD), F32)
    acc2[24] = jnp.zeros((HD, HD), F32)
    lse[24] = jnp.full((1, HD), NEG, F32)
    lse2[24] = jnp.full((1, HD), NEG, F32)
    same_head = iota((HD, HD), 0) // 64 == (iota((HD, HD), 1) % 64) // 32
    left = iota((HD, HD), 1) < 64
    left1 = lane1 < 64
    left64 = lane < 64
    zeros6 = jnp.zeros((6, HD), F32)

    def prompt_part(hi):
        def page(n, src, i):
            d = dests[first_row + n]
            zl, dy, dx = d // 16, (d // 4) % 4, d % 4
            part = jnp.concatenate([qa[hi][dx, dy, zl], qb[hi][dy, dx, zl]], axis=0)
            swap = jnp.concatenate([part[:, 64:], part[:, :64]], axis=1)
            asked = jnp.concatenate([jnp.where(left64, part, swap), jnp.where(left64, swap, part)], axis=0)
            score = jnp.where(same_head, dot_nn(pages[src, hi, i, 0].reshape(HD, HD), asked) * SCALE, NEG)
            top = jnp.max(score, axis=0, keepdims=True)
            weight = jnp.exp(score - top).astype(BF16)
            total = jnp.sum(weight.astype(F32), axis=0, keepdims=True)
            acc[n] = dot_tn(pages[src, hi, i, 1].reshape(HD, HD), weight) / total
            lse[n] = top + jnp.log(total)

        def page_step(i, carry):
            for src in range(2):
                for more in range(UNROLL):
                    page(src * 12 + i * UNROLL + more, src, i * UNROLL + more)
            return carry

        lax.fori_loop(0, 12 // UNROLL, page_step, 0)

        def join_step(i, carry):
            for more in range(4):
                n = i * 4 + more
                d = dests[first_row + n]
                first = index[0, d]
                other = jnp.where(first == n, index[1, d], first)
                weights, joined = shares([lse[n], lse[other]])
                acc2[n] = acc[n] * weights[0] + acc[other] * weights[1]
                lse2[n] = joined
            return carry

        lax.fori_loop(0, 6, join_step, 0)

        for zp in range(2):
            def place_step(dy, carry):
                for dx in range(4):
                    d = zp * 32 + dy * 4 + dx
                    one, two = index[0, d], index[0, d + 16]
                    block = jnp.where(left, acc2[one], acc2[two]).astype(BF16)
                    stat = jnp.where(left1, lse2[one], lse2[two])
                    sa[hi, dx, dy * 2 + zp] = block[:64]
                    sb[hi, dy, dx * 2 + zp] = block[64:]
                    la[hi, dx, pl.ds(dy * 2 + zp, 1), :] = stat
                    lb[hi, dy, pl.ds(dx * 2 + zp, 1), :] = stat
                return carry

            lax.fori_loop(0, 4, place_step, 0)

    def send_first(hi):
        sent = []
        for k in (1, 0, 2):
            to_x, to_y = (x + k + 1) % 4, (y + k + 1) % 4
            for m, (src, dst, peer) in enumerate((
                (sa.at[hi, to_x], ra.at[hi, k], x_peers[k]),
                (sb.at[hi, to_y], rb.at[hi, k], y_peers[k]),
                (la.at[hi, to_x], rla.at[hi, k], x_peers[k]),
                (lb.at[hi, to_y], rlb.at[hi, k], y_peers[k]),
            )):
                sent.append(remote(src, dst, r1_ssem.at[hi, m, k], r1_rsem.at[hi, m, k], peer))
        for copy in sent:
            copy.start()
        return sent

    def merge_first(hi):
        for mine_s, mine_l, got_s, got_l, where, next_s, next_l in (
            (sa, la, ra, rla, x, sa2, la2), (sb, lb, rb, rlb, y, sb2, lb2)
        ):
            weights, joined = shares([mine_l[hi, where]] + [got_l[hi, k] for k in range(3)])
            for t in range(8):
                block = mine_s[hi, where, t].astype(F32) * weights[0][t : t + 1]
                for k in range(3):
                    block = block + got_s[hi, k, t].astype(F32) * weights[k + 1][t : t + 1]
                next_s[hi, t // 2, t % 2] = block.astype(BF16)
            for group in range(4):
                next_l[hi, group] = jnp.concatenate([joined[group * 2 : group * 2 + 2], zeros6], axis=0)

    def send_second(hi):
        sent = []
        for k in (1, 0, 2):
            to_x, to_y = (x + k + 1) % 4, (y + k + 1) % 4
            for m, (src, dst, peer) in enumerate((
                (sa2.at[hi, to_y], ra2.at[hi, k], y_peers[k]),
                (sb2.at[hi, to_x], rb2.at[hi, k], x_peers[k]),
                (la2.at[hi, to_y], rla2.at[hi, k], y_peers[k]),
                (lb2.at[hi, to_x], rlb2.at[hi, k], x_peers[k]),
            )):
                sent.append(remote(src, dst, r2_ssem.at[hi, m, k], r2_rsem.at[hi, m, k], peer))
        for copy in sent:
            copy.start()
        return sent

    def merge_second(hi):
        both = []
        for mine_s, mine_l, got_s, got_l, where in ((sa2, la2, ra2, rla2, y), (sb2, lb2, rb2, rlb2, x)):
            weights, joined = shares([mine_l[hi, where]] + [got_l[hi, k] for k in range(3)])
            blocks = []
            for zp in range(2):
                block = mine_s[hi, where, zp].astype(F32) * weights[0][zp : zp + 1]
                for k in range(3):
                    block = block + got_s[hi, k, zp].astype(F32) * weights[k + 1][zp : zp + 1]
                blocks.append(block)
            both.append((blocks, joined))
        for zp in range(2):
            a, b = both[0][0][zp], both[1][0][zp]
            s3[hi * 4 + zp * 2] = jnp.where(left64, a, pltpu.roll(b, 64, 1)).astype(BF16)
            s3[hi * 4 + zp * 2 + 1] = jnp.where(left64, pltpu.roll(a, 64, 1), b).astype(BF16)
            a, b = both[0][1], both[1][1]
            l3[hi * 4 + zp * 2] = jnp.where(lane8 < 64, a, pltpu.roll(b, 64, 1))[zp : zp + 1]
            l3[hi * 4 + zp * 2 + 1] = jnp.where(lane8 < 64, pltpu.roll(a, 64, 1), b)[zp : zp + 1]

    for copy in g3[0][1] + g3[0][2]:
        copy.wait_recv()
    prompt_part(0)
    r1_low = send_first(0)
    for copy in g3[1][0] + g3[1][2]:
        copy.wait_recv()
    prompt_part(1)
    r1_high = send_first(1)
    for copy in gz + g2[0] + g2[1] + g3[0][0] + g3[0][1] + g3[0][2] + g3[1][0] + g3[1][1] + g3[1][2] + mig + core_copies:
        copy.wait_send()
    for copy in ret:
        copy.wait_recv()
    back = [ret_rcv[bit, s].astype(F32) for s in range(4)]
    for j in range(4):
        for s in range(4):
            out[j, s] = jnp.where(my_slot == j, back[s], ret_loc[j, s].astype(F32)).astype(BF16)
    for copy in r1_low:
        copy.wait_recv()
    merge_first(0)
    r2_low = send_second(0)
    for copy in r1_high:
        copy.wait_recv()
    merge_first(1)
    r2_high = send_second(1)
    for copy in r2_low:
        copy.wait_recv()
    merge_second(0)
    for copy in r2_high:
        copy.wait_recv()
    merge_second(1)

    rz = []
    for k in (3, 2, 4, 1, 5, 0, 6):
        to = (z + k + 1) % 8
        rz.append(remote(s3.at[to], r3.at[k], rz_ssem.at[0, k], rz_rsem.at[0, k], z_peers[k]))
        rz.append(remote(l3.at[to], rl3.at[k], rz_ssem.at[1, k], rz_rsem.at[1, k], z_peers[k]))
    for copy in rz:
        copy.start()
    for copy in r1_low + r1_high + r2_low + r2_high + ret:
        copy.wait_send()
    for copy in rz:
        copy.wait_recv()
    weights, _ = shares([new_lse, l3[z]] + [rl3[k] for k in range(7)])
    block = new_acc * weights[0] + s3[z].astype(F32) * weights[1]
    for k in range(7):
        block = block + r3[k].astype(F32) * weights[k + 2]
    flat = jnp.concatenate([block, block], axis=0).T
    here = jnp.where(left64, flat[:64], flat[64:])
    for s in range(4):
        out[4, s] = jnp.concatenate([here[s * 8 : s * 8 + 8], here[32 + s * 8 : 40 + s * 8]], axis=0).astype(BF16)
    for copy in rz:
        copy.wait_send()


def per_device(
    pool_kv, block_table, context_len, partner, mig_slot, prompt_kv, prompt_dest, queries, step_kv
):
    vmem = pl.BlockSpec(memory_space=pltpu.VMEM)
    hbm = pl.BlockSpec(memory_space=pltpu.HBM)
    sem = lambda *shape: pltpu.SemaphoreType.DMA(shape)
    V = pltpu.VMEM
    return pl.pallas_call(
        body,
        out_shape=jax.ShapeDtypeStruct((5, 4, 16, HD), BF16),
        in_specs=[hbm] * 11,
        out_specs=vmem,
        scratch_shapes=[
            pltpu.SMEM((3072,), jnp.int32),
            pltpu.SMEM((4, 64), jnp.int32),
            pltpu.SMEM((64,), jnp.int32),
            pltpu.SMEM((64,), jnp.int32),
            pltpu.SMEM((4, 24), jnp.int32),
            V((24, HD), jnp.int32),
            V((1, HD), F32),
            V((5, 4, 16, HD), BF16),
            V((5, 16, HD), BF16),
            V((48, 2, 2, 64, HD), BF16),
            V((2, 2, 12, 2, 2, 64, HD), BF16),
            V((12, 8, HD), F32),
            V((8, HD), jnp.int32),
            pltpu.SMEM((8, HD), jnp.int32),
            V((4, 80, HD), BF16),
            V((80, HD), BF16),
            V((3, 80, HD), BF16),
            V((4, 4, 16, HD), BF16),
            V((4, 16, HD), BF16),
            V((3, 4, 16, HD), BF16),
            V((8, 64, HD), BF16),
            V((4, 4, 4, 32, HD), BF16),
            V((4, 4, 4, 32, HD), BF16),
            V((4, 4, 4, 32, HD), BF16),
            V((4, 4, 4, 32, HD), BF16),
            V((25, HD, HD), F32),
            V((25, 1, HD), F32),
            V((25, HD, HD), F32),
            V((25, 1, HD), F32),
            V((2, 4, 8, 64, HD), BF16),
            V((2, 4, 8, 64, HD), BF16),
            V((2, 4, 8, HD), F32),
            V((2, 4, 8, HD), F32),
            V((2, 3, 8, 64, HD), BF16),
            V((2, 3, 8, 64, HD), BF16),
            V((2, 3, 8, HD), F32),
            V((2, 3, 8, HD), F32),
            V((2, 4, 2, 64, HD), BF16),
            V((2, 4, 2, 64, HD), BF16),
            V((2, 4, 8, HD), F32),
            V((2, 4, 8, HD), F32),
            V((2, 3, 2, 64, HD), BF16),
            V((2, 3, 2, 64, HD), BF16),
            V((2, 3, 8, HD), F32),
            V((2, 3, 8, HD), F32),
            V((8, 64, HD), BF16),
            V((8, 1, HD), F32),
            V((7, 64, HD), BF16),
            V((7, 1, HD), F32),
            sem(9), sem(4), sem(2), sem(2), sem(3), sem(3), sem(3), sem(3),
            sem(7), sem(7), sem(2, 2, 3), sem(2, 2, 3), sem(2, 2, 3), sem(2, 2, 3),
            sem(2, 4, 3), sem(2, 4, 3), sem(2, 4, 3), sem(2, 4, 3), sem(2, 7), sem(2, 7),
        ],
        compiler_params=pltpu.CompilerParams(
            collective_id=0, has_side_effects=True, vmem_limit_bytes=60 * 1024 * 1024
        ),
    )(
        prompt_dest.reshape(-1), context_len.T, partner, mig_slot, block_table,
        prompt_dest.reshape(24, HD), jnp.asarray(rope_row()), queries, step_kv.reshape(5, 16, HD),
        pool_kv, prompt_kv,
    )


def solution(mesh):
    placed = (
        P("inst", None, "tp", None, None),
        P("inst", None),
        P(),
        P(),
        P(),
        P(("inst", "tp"), None, None, None, None),
        P(),
        P("inst", None, "tp", None),
        P("inst", None, None, "tp", None),
    )
    return jax.shard_map(
        per_device,
        mesh=mesh,
        in_specs=placed,
        out_specs=P("inst", None, "tp", None),
        check_vma=False,
    )
```
